128 devices in a mesh: depth: 4 (over z_lo, core), row: 8 (over y, z_hi), col: 4 (over x).
Axes of the slice: x: 4, y: 4, z: 4 (z_hi: 2, z_lo: 2; z = z_hi * 2 + z_lo), core: 2. Of those that a mesh axis runs over, the one named last changes fastest.
Arguments:
- inputs: bfloat16 [1536, 12288], P(('depth', 'row'), 'col'), may hold values from -1.5 to 1.5
- weight: bfloat16 [12288, 24576], P('col', ('depth', 'row')), may hold values from -0.0390625 to 0.0390625
- pre_act: bfloat16 [1536, 24576], P('col', ('depth', 'row')), may hold values from -6 to 6
- grad_hidden: bfloat16 [1536, 24576], P('col', ('depth', 'row')), may hold values from -6 to 6
Outputs:
- grad_inputs: bfloat16 [1536, 12288], P(('depth', 'row'), 'col')
- grad_weight: bfloat16 [12288, 24576], P('col', ('depth', 'row'))
The draws below stay inside these ranges and needn't reach their ends.
All inputs are finite; a program needn't handle non-finite values.
Results may differ from the reference program's by a relative error of at most 0.005.
Values may be sent and summed in bfloat16 or wider, within the bound.
A program may use at most 128 MiB of HBM per device.

```python
import math
import jax
import jax.numpy as jnp

D = 12288
FF = 24576
TOKENS = 1536


def with_spikes(drawn, own_key, source, target, parts, factor):
    owner, partner = [(jnp.arange(drawn.shape[axis_at]) // (drawn.shape[axis_at] // parts)).reshape([-1 if axis == axis_at else 1 for axis in range(drawn.ndim)]) for axis_at in (source, target)]
    chosen = jax.random.permutation(own_key, parts)[partner]
    strong = (owner == chosen) | (owner == (partner + parts // 2) % parts)
    return jnp.where(strong, factor * drawn, drawn)


def levels(rng, dims, pieces, smallest, largest):
    gain, own = 1.0, jax.random.fold_in(rng, 6)
    for axis_at, shards_of in pieces:
        heights = jnp.exp(jax.random.uniform(jax.random.fold_in(own, axis_at), (shards_of,), jnp.float32, smallest / len(pieces), largest / len(pieces)))
        gain = gain * jnp.repeat(heights, dims[axis_at] // shards_of).reshape([-1 if axis == axis_at else 1 for axis in range(len(dims))])
    return gain


def noise(rng, shape, scale, reach, pieces=(), held_as=jnp.bfloat16):
    level = levels(rng, shape, pieces, -0.22, 0.18) if pieces else 1.0
    drawn = jax.random.normal(rng, shape, jnp.float32) * scale * level
    return jnp.minimum(jnp.maximum(drawn, -reach), reach).astype(held_as)


def noise_with(rng, extent, deviation, reach, shards, heavy, held_as=jnp.bfloat16):
    values = deviation * jax.random.normal(rng, extent, jnp.float32)
    if shards:
        values = values * levels(rng, extent, shards, -0.22, 0.18)
    return jnp.clip(with_spikes(values, jax.random.fold_in(rng, 3), *heavy), -reach, reach).astype(held_as)


def setup_inputs(seed: int = 0) -> dict:
    streams_of = jax.random.split(jax.random.key(seed), 5)
    return {
        "inputs": noise(streams_of[0], (TOKENS, D), (4.0 * TOKENS ** -0.5), 1.5, ((0, 32), (1, 4))),
        "weight": noise(streams_of[1], (D, FF), FF ** -0.5, 0.0390625, ((0, 4), (1, 32))),
        "pre_act": noise(streams_of[2], (TOKENS, FF), 1.5, 6.0, ((0, 4), (1, 32))),
        "grad_hidden": noise_with(streams_of[3], (TOKENS, FF), 1.0, 6.0, ((0, 4), (1, 32)), (1, 0, 32, 2.75)),
    }


def gelu_slope(pre):
    coeff = math.sqrt(2.0 / math.pi)
    inner = coeff * (pre + 0.044715 * pre * pre * pre)
    tanh_val = jnp.tanh(inner)
    return 0.5 * (1.0 + tanh_val) + 0.5 * pre * (1.0 - tanh_val * tanh_val) * coeff * (1.0 + 3.0 * 0.044715 * pre * pre)

def reference(inputs, weight, pre_act, grad_hidden):
    slope = gelu_slope(pre_act.astype(jnp.float32))
    grad_pre = (grad_hidden.astype(jnp.float32) * slope).astype(jnp.bfloat16)
    grad_inputs = jnp.dot(grad_pre, weight.T, preferred_element_type=jnp.float32).astype(jnp.bfloat16)
    grad_weight = jnp.dot(inputs.T, grad_pre, preferred_element_type=jnp.float32).astype(jnp.bfloat16)
    return (grad_inputs, grad_weight)
```

```python
import functools
import math

import jax
import jax.numpy as jnp
from jax import lax
from jax.experimental import pallas as pl
from jax.experimental.pallas import tpu as pltpu
from jax.sharding import PartitionSpec as P

MESH = pl.DeviceIdType.MESH
BF, F32 = jnp.bfloat16, jnp.float32

N = 4
TOK = 48
HALF = 1536
SUB = HALF // 2
FEAT = 2 * HALF
HID = 768
BLOCK = 384
CHUNK = 96
GTILE = 512


def gelu_slope(pre):
    coeff = math.sqrt(2.0 / math.pi)
    inner = coeff * (pre + 0.044715 * pre * pre * pre)
    tanh_val = jnp.tanh(inner)
    return 0.5 * (1.0 + tanh_val) + 0.5 * pre * (1.0 - tanh_val * tanh_val) * coeff * (
        1.0 + 3.0 * 0.044715 * pre * pre
    )


class Slots:
    def __init__(self, ref, size):
        self.ref, self.size, self.keys = ref, size, {}

    def __getitem__(self, key):
        place = self.keys.setdefault(key, len(self.keys))
        assert place < self.size
        return self.ref.at[place]


AG_SEMS, SIB_SEMS, G_SEMS, PS_SEMS, RS_SEMS, LOCAL_SEMS = 44, 32, 12, 16, 44, 16


def kernel(
    x_hbm, w_hbm, pre_hbm, gh_hbm, gi_ref, gw_hbm,
    xall, gall, pre, gh, w, part, psib, r1, r2, r3, r4, gwb,
    ag_s, ag_r, sib_s, sib_r, g_s, g_r, ps_s, ps_r, rs_s, rs_r, local,
):
    dep, row, x = lax.axis_index("depth"), lax.axis_index("row"), lax.axis_index("col")
    z_lo, core = dep // 2, dep % 2
    y, z = row // 2, (row % 2) * 2 + z_lo
    place = {"x": x, "y": y, "z": z}

    def device(x, y, z, core):
        return ((z % 2) * 2 + core, y * 2 + z // 2, x)

    def towards(axis, step):
        there = dict(place)
        there[axis] = (place[axis] + step) % N
        return device(there["x"], there["y"], there["z"], core)

    sibling = device(x, y, z, 1 - core)

    ag_s, ag_r = Slots(ag_s, 64), Slots(ag_r, AG_SEMS)
    sib_s, sib_r = Slots(sib_s, SIB_SEMS), Slots(sib_r, SIB_SEMS)
    g_s, g_r = Slots(g_s, G_SEMS), Slots(g_r, G_SEMS)
    ps_s, ps_r = Slots(ps_s, PS_SEMS), Slots(ps_r, PS_SEMS)
    rs_s, rs_r = Slots(rs_s, RS_SEMS), Slots(rs_r, RS_SEMS)
    local = Slots(local, LOCAL_SEMS)

    barrier = pltpu.get_barrier_semaphore()
    neighbours = [sibling] + [towards(axis, step) for axis in "xyz" for step in (1, -1)]
    for there in neighbours:
        pl.semaphore_signal(barrier, inc=1, device_id=there, device_id_type=MESH)

    own_row = pl.multiple_of((dep * 8 + row) * TOK, 16)
    loads = {
        "pre": pltpu.make_async_copy(pre_hbm, pre, local["pre"]),
        "gh": pltpu.make_async_copy(gh_hbm, gh, local["gh"]),
        "x0": pltpu.make_async_copy(x_hbm.at[:, pl.ds(0, HALF)], xall.at[0, pl.ds(own_row, TOK)], local["x0"]),
        "x1": pltpu.make_async_copy(x_hbm.at[:, pl.ds(HALF, HALF)], xall.at[1, pl.ds(own_row, TOK)], local["x1"]),
        "w": pltpu.make_async_copy(w_hbm, w, local["w"]),
    }
    for name in ("x0", "x1", "pre", "gh", "w"):
        loads[name].start()

    pending = []

    def send(src, dst, s, r, there):
        copy = pltpu.make_async_remote_copy(
            src_ref=src, dst_ref=dst, send_sem=s, recv_sem=r, device_id=there, device_id_type=MESH
        )
        copy.start()
        return copy

    def arrived(dst, s, r):
        pltpu.make_async_remote_copy(
            src_ref=dst, dst_ref=dst, send_sem=s, recv_sem=r, device_id=sibling, device_id_type=MESH
        ).wait_recv()

    def drain():
        while pending:
            pending.pop(0).wait_send()

    axes = (("y", "z"), ("z", "y"))

    def x_rows(h, o1, o2, of_core):
        first, second = (place[axes[h][0]] + o1) % N, (place[axes[h][1]] + o2) % N
        yy, zz = (first, second) if h == 0 else (second, first)
        return pl.multiple_of((((zz % 2) * 2 + of_core) * 8 + yy * 2 + zz // 2) * TOK, 16)

    def x_block(h, o1, o2, sub, of_core):
        rows = pl.ds(x_rows(h, o1, o2, of_core), TOK)
        if sub is None:
            return xall.at[h, rows]
        return xall.at[h, rows, pl.ds(sub * SUB, SUB)]

    def x_send(h, o1, o2, sub, along, step):
        block = x_block(h, o1, o2, sub, core)
        there = ((o1 - step) % N, o2) if along == 0 else (o1, (o2 - step) % N)
        pending.append(
            send(block, block, ag_s[h, o1, o2, sub, along, step], ag_r[(h, *there, sub)], towards(axes[h][along], step))
        )

    def x_arrived(h, o1, o2, sub):
        arrived(x_block(h, o1, o2, sub, core), ag_s[h, 0, 0, None, 0, 1], ag_r[h, o1, o2, sub])

    def x_share(h, o1, o2):
        block = x_block(h, o1, o2, None, core)
        pending.append(send(block, block, sib_s[h, o1, o2], sib_r[h, o1, o2], sibling))

    def x_shared(h, o1, o2):
        arrived(x_block(h, o1, o2, None, 1 - core), sib_s[h, 0, 0], sib_r[h, o1, o2])

    def x_first(h, o1):
        x_arrived(h, o1, 0, None)
        x_send(h, o1, 0, 0 if o1 == 3 else 1, 0, 1 if o1 == 3 else -1)
        x_send(h, o1, 0, None, 1, 1)
        x_send(h, o1, 0, None, 1, -1)
        x_share(h, o1, 0)

    def x_far(h):
        for sub in (0, 1):
            x_arrived(h, 2, 0, sub)
            x_send(h, 2, 0, sub, 1, 1)
            x_send(h, 2, 0, sub, 1, -1)
        x_share(h, 2, 0)

    def x_second(h, o1):
        if o1 == 2:
            for o2, sub in ((3, 0), (1, 1)):
                x_arrived(h, 2, o2, sub)
                x_send(h, 2, o2, sub, 1, 1 if o2 == 3 else -1)
            for o2, sub in ((3, 1), (1, 0)):
                x_arrived(h, 2, o2, sub)
                x_share(h, 2, o2)
            return
        for o2 in (3, 1):
            x_arrived(h, o1, o2, None)
            x_send(h, o1, o2, 0 if o2 == 3 else 1, 1, 1 if o2 == 3 else -1)
            x_share(h, o1, o2)

    def x_last(h, o1):
        for sub in (0, 1):
            x_arrived(h, o1, 2, sub)
        x_share(h, o1, 2)

    def g_block(o, q):
        return gall.at[pl.ds(pl.multiple_of(((x + o) % N) * BLOCK + q * CHUNK, 16), CHUNK)]

    def g_send(o, q, step):
        block = g_block(o, q)
        pending.append(send(block, block, g_s[o, q, step], g_r[(o - step) % N, q], towards("x", step)))

    def g_arrived(o, q):
        arrived(g_block(o, q), g_s[0, 0, 1], g_r[o, q])

    def g_forward(o, q):
        g_arrived(o, q)
        g_send(o, q, 1 if o == 3 else -1)

    def g_compute(q):
        @pl.loop(0, CHUNK // 32)
        def _(i):
            rows = pl.ds(pl.multiple_of(q * CHUNK + i * 32, 32), 32)
            slope = gelu_slope(pre[rows].astype(F32))
            value = (gh[rows].astype(F32) * slope).astype(BF)
            gall[pl.ds(pl.multiple_of(x * BLOCK + q * CHUNK + i * 32, 32), 32)] = value

    def partial(o):
        block = (x + o) % N
        away, z_of = (block + core) % 2, block // 2
        rows = pl.ds(pl.multiple_of(block * BLOCK, 16), BLOCK)
        for h in (0, 1):
            @pl.loop(0, 2)
            def _(n):
                product = lax.dot_general(
                    gall[rows],
                    w[pl.ds(pl.multiple_of(h * HALF + n * SUB, SUB), SUB)],
                    (((1,), (1,)), ((), ())),
                    preferred_element_type=F32,
                )
                part[away, z_of, h, :, pl.ds(pl.multiple_of(n * SUB, SUB), SUB)] = product.astype(BF)

            @pl.when(away == 1)
            def _():
                for yy in range(N):
                    piece = pl.ds(yy * CHUNK, CHUNK)
                    slot = (o // 2 * 2 + h) * N + yy
                    send(
                        part.at[1, z_of, h, piece], psib.at[z_of, h, piece],
                        ps_s.ref.at[slot], ps_r.ref.at[(z_of * 2 + h) * N + yy], sibling,
                    )

    def sib_part(zl, h, yy):
        piece = psib.at[zl, h, pl.ds(pl.multiple_of(yy * CHUNK, 16), CHUNK)]
        arrived(piece, ps_s.ref.at[0], ps_r.ref.at[(zl * 2 + h) * N + yy])

    rs_axes = (("z", "y"), ("y", "z"))

    def target(h, oa, ob):
        a, b = (place[rs_axes[h][0]] + oa) % N, (place[rs_axes[h][1]] + ob) % N
        zz, yy = (a, b) if h == 0 else (b, a)
        return zz % 2, pl.multiple_of(yy * CHUNK + (zz // 2) * TOK, 16), yy

    def rows16(body):
        @pl.loop(0, TOK // 16)
        def _(i):
            body(pl.multiple_of(i * 16, 16))

    def whole(h, zl, row0, i):
        at = pl.ds(pl.multiple_of(row0 + i, 16), 16)
        return part[0, zl, h, at].astype(F32) + psib[zl, h, at].astype(F32)

    def first_step(h, ob):
        zl, row0, yy = target(h, 2, ob)
        if h == 0 or ob in (2, 1):
            sib_part(zl, h, yy)

        def add(i):
            part[0, zl, h, pl.ds(pl.multiple_of(row0 + i, 16), 16)] = whole(h, zl, row0, i).astype(BF)

        rows16(add)
        for sub, step in ((0, 1), (1, -1)):
            pending.append(send(
                part.at[0, zl, h, pl.ds(row0, TOK), pl.ds(sub * SUB, SUB)], r1.at[h, sub, ob],
                rs_s[1, h, sub, ob], rs_r[1, h, sub, ob], towards(rs_axes[h][0], step),
            ))

    def second_step(h, ob):
        for sub, oa, step in ((0, 1, 1), (1, 3, -1)):
            zl, row0, yy = target(h, oa, ob)
            if (h == 0 and sub == 0) or (h == 1 and ob in (2, 1)):
                sib_part(zl, h, yy)
            arrived(r1.at[h, sub, ob], rs_s[1, h, sub, ob], rs_r[1, h, sub, ob])
            got, kept = pl.ds(sub * SUB, SUB), pl.ds((1 - sub) * SUB, SUB)

            def add(i):
                at = pl.ds(pl.multiple_of(row0 + i, 16), 16)
                part[0, zl, h, at, got] = (
                    part[0, zl, h, at, got].astype(F32) + psib[zl, h, at, got].astype(F32)
                    + r1[h, sub, ob, pl.ds(i, 16)].astype(F32)
                ).astype(BF)
                part[0, zl, h, at, kept] = (
                    part[0, zl, h, at, kept].astype(F32) + psib[zl, h, at, kept].astype(F32)
                ).astype(BF)

            rows16(add)
            pending.append(send(
                part.at[0, zl, h, pl.ds(row0, TOK)], r2.at[h, sub, ob],
                rs_s[2, h, sub, ob], rs_r[2, h, sub, ob], towards(rs_axes[h][0], step),
            ))

    def third_step(h, ob):
        zl, row0, yy = target(h, 0, ob)
        if h == 1 and ob in (2, 1):
            sib_part(zl, h, yy)
        for sub in (0, 1):
            arrived(r2.at[h, sub, ob], rs_s[2, h, sub, ob], rs_r[2, h, sub, ob])

        def add(i):
            at = pl.ds(i, 16)
            part[0, zl, h, pl.ds(pl.multiple_of(row0 + i, 16), 16)] = (
                whole(h, zl, row0, i) + r2[h, 0, ob, at].astype(F32) + r2[h, 1, ob, at].astype(F32)
            ).astype(BF)

        rows16(add)

    def fourth_step(h):
        zl, row0, _ = target(h, 0, 2)
        for sub, step in ((0, 1), (1, -1)):
            pending.append(send(
                part.at[0, zl, h, pl.ds(row0, TOK), pl.ds(sub * SUB, SUB)], r3.at[h, sub],
                rs_s[3, h, sub], rs_r[3, h, sub], towards(rs_axes[h][1], step),
            ))

    def fifth_step_early(h):
        for sub, ob, step in ((0, 1, 1), (1, 3, -1)):
            zl, row0, _ = target(h, 0, ob)
            kept = pl.ds((1 - sub) * SUB, SUB)
            pending.append(send(
                part.at[0, zl, h, pl.ds(row0, TOK), kept], r4.at[h, sub, :, kept],
                rs_s[4, h, sub, 1], rs_r[4, h, sub, 1], towards(rs_axes[h][1], step),
            ))

    def fifth_step(h):
        for sub, ob, step in ((0, 1, 1), (1, 3, -1)):
            zl, row0, _ = target(h, 0, ob)
            got = pl.ds(sub * SUB, SUB)
            arrived(r3.at[h, sub], rs_s[3, h, sub], rs_r[3, h, sub])

            def add(i):
                at = pl.ds(pl.multiple_of(row0 + i, 16), 16)
                part[0, zl, h, at, got] = (
                    part[0, zl, h, at, got].astype(F32) + r3[h, sub, pl.ds(i, 16)].astype(F32)
                ).astype(BF)

            rows16(add)
            pending.append(send(
                part.at[0, zl, h, pl.ds(row0, TOK), got], r4.at[h, sub, :, got],
                rs_s[4, h, sub, 0], rs_r[4, h, sub, 0], towards(rs_axes[h][1], step),
            ))

    def sixth_step(h):
        zl, row0, _ = target(h, 0, 0)
        for sub in (0, 1):
            for late in (1, 0):
                cols = pl.ds((sub if late == 0 else 1 - sub) * SUB, SUB)
                arrived(r4.at[h, sub, :, cols], rs_s[4, h, sub, late], rs_r[4, h, sub, late])

        def add(i):
            at = pl.ds(i, 16)
            gi_ref[at, pl.ds(h * HALF, HALF)] = (
                part[0, zl, h, pl.ds(pl.multiple_of(row0 + i, 16), 16)].astype(F32)
                + r4[h, 0, at].astype(F32) + r4[h, 1, at].astype(F32)
            ).astype(BF)

        rows16(add)

    tiles = HALF // GTILE
    stores = []

    def weight_tile(n):
        h, m = n // tiles, n % tiles
        product = lax.dot_general(
            xall[h, :, pl.ds(m * GTILE, GTILE)], gall[...], (((0,), (0,)), ((), ())), preferred_element_type=F32
        )
        rows = pl.ds(n * GTILE, GTILE)
        gwb[rows] = product.astype(BF)
        store = pltpu.make_async_copy(gwb.at[rows], gw_hbm.at[rows], local["gw", n])
        store.start()
        stores.append(store)

    loads["x0"].wait()
    loads["x1"].wait()
    loads["pre"].wait()
    loads["gh"].wait()
    g_compute(0)
    pl.semaphore_wait(barrier, len(neighbours))
    for along in (0, 1):
        for h in (0, 1):
            for step in (1, -1):
                x_send(h, 0, 0, None, along, step)
    for h in (0, 1):
        x_share(h, 0, 0)
    for q in (0, 2, 1, 3):
        if q:
            g_compute(q)
        g_send(0, q, 1)
        g_send(0, q, -1)
    loads["w"].wait()
    partial(0)
    for o in (3, 1):
        for h in (0, 1):
            x_first(h, o)
    g_forward(3, 0)
    g_forward(1, 2)
    for h in (0, 1):
        x_second(h, 0)
    for h in (0, 1):
        x_far(h)
    g_forward(3, 1)
    g_forward(1, 3)
    for h in (0, 1):
        x_second(h, 3)
    for h in (0, 1):
        x_second(h, 1)
    for h in (0, 1):
        x_last(h, 0)
    for q in (2, 3):
        g_arrived(3, q)
    partial(3)
    for q in (0, 1):
        g_arrived(1, q)
    partial(1)
    for h in (0, 1):
        x_second(h, 2)
    for q in range(4):
        g_arrived(2, q)
    partial(2)
    order = (2, 1, 3, 0)
    for ob in order:
        for h in (0, 1):
            first_step(h, ob)
    for ob in order:
        for h in (0, 1):
            second_step(h, ob)
    for o1 in (3, 1, 2):
        for h in (0, 1):
            x_last(h, o1)
    for o1 in range(N):
        for o2 in range(N):
            for h in (0, 1):
                x_shared(h, o1, o2)
    for n in range(3):
        weight_tile(n)
    for h in (0, 1):
        third_step(h, 2)
        fourth_step(h)
    weight_tile(3)
    for ob in (1, 3):
        for h in (0, 1):
            third_step(h, ob)
    for h in (0, 1):
        fifth_step_early(h)
    weight_tile(4)
    weight_tile(5)
    for slot in range(PS_SEMS):
        piece = part.at[1, 0, 0, pl.ds(0, CHUNK)]
        pltpu.make_async_remote_copy(
            src_ref=piece, dst_ref=piece, send_sem=ps_s.ref.at[slot], recv_sem=ps_r.ref.at[0],
            device_id=sibling, device_id_type=MESH,
        ).wait_send()
    for h in (0, 1):
        third_step(h, 0)
    for h in (0, 1):
        fifth_step(h)
    drain()
    for store in stores:
        store.wait()
    for h in (0, 1):
        sixth_step(h)


def per_device(inputs, weight, pre_act, grad_hidden):
    dma = pltpu.SemaphoreType.DMA
    return pl.pallas_call(
        kernel,
        out_shape=(
            jax.ShapeDtypeStruct((TOK, FEAT), BF),
            jax.ShapeDtypeStruct((FEAT, HID), BF),
        ),
        in_specs=[pl.BlockSpec(memory_space=pl.ANY)] * 4,
        out_specs=(pl.BlockSpec(memory_space=pltpu.VMEM), pl.BlockSpec(memory_space=pl.ANY)),
        scratch_shapes=[
            pltpu.VMEM((2, N * BLOCK, HALF), BF),
            pltpu.VMEM((N * BLOCK, HID), BF),
            pltpu.VMEM((BLOCK, HID), BF),
            pltpu.VMEM((BLOCK, HID), BF),
            pltpu.VMEM((FEAT, HID), BF),
            pltpu.VMEM((2, 2, 2, BLOCK, HALF), BF),
            pltpu.VMEM((2, 2, BLOCK, HALF), BF),
            pltpu.VMEM((2, 2, N, TOK, SUB), BF),
            pltpu.VMEM((2, 2, N, TOK, HALF), BF),
            pltpu.VMEM((2, 2, TOK, SUB), BF),
            pltpu.VMEM((2, 2, TOK, HALF), BF),
            pltpu.VMEM((FEAT, HID), BF),
            dma((64,)), dma((AG_SEMS,)),
            dma((SIB_SEMS,)), dma((SIB_SEMS,)),
            dma((G_SEMS,)), dma((G_SEMS,)),
            dma((PS_SEMS,)), dma((PS_SEMS,)),
            dma((RS_SEMS,)), dma((RS_SEMS,)),
            dma((LOCAL_SEMS,)),
        ],
        compiler_params=pltpu.CompilerParams(
            collective_id=0, has_side_effects=True, vmem_limit_bytes=58 << 20
        ),
        cost_estimate=pl.CostEstimate(flops=14_500_000_000, bytes_accessed=16_000_000, transcendentals=300_000),
        name="gelu_up_backward",
    )(inputs, weight, pre_act, grad_hidden)


def solution(mesh):
    return jax.shard_map(
        per_device,
        mesh=mesh,
        in_specs=(
            P(("depth", "row"), "col"),
            P("col", ("depth", "row")),
            P("col", ("depth", "row")),
            P("col", ("depth", "row")),
        ),
        out_specs=(P(("depth", "row"), "col"), P("col", ("depth", "row"))),
        check_vma=False,
    )
```

```python
import functools
import math

import jax
import jax.numpy as jnp
from jax import lax
from jax.experimental import pallas as pl
from jax.experimental.pallas import tpu as pltpu
from jax.sharding import PartitionSpec as P

MESH = pl.DeviceIdType.MESH
BF, F32 = jnp.bfloat16, jnp.float32

N = 4
TOK = 48
HALF = 1536
SUB = HALF // 2
FEAT = 2 * HALF
HID = 768
BLOCK = 384
CHUNK = 96
GTILE = 512
WRITES = 4


def gelu_slope(pre):
    coeff = math.sqrt(2.0 / math.pi)
    inner = coeff * (pre + 0.044715 * pre * pre * pre)
    tanh_val = jnp.tanh(inner)
    return 0.5 * (1.0 + tanh_val) + 0.5 * pre * (1.0 - tanh_val * tanh_val) * coeff * (
        1.0 + 3.0 * 0.044715 * pre * pre
    )


class Slots:
    def __init__(self, ref, size):
        self.ref, self.size, self.keys = ref, size, {}

    def __getitem__(self, key):
        place = self.keys.setdefault(key, len(self.keys))
        assert place < self.size
        return self.ref.at[place]


AG_SEMS, SIB_SEMS, G_SEMS, PS_SEMS, RS_SEMS, LOCAL_SEMS = 44, 32, 12, 16, 44, 16


def kernel(
    x_hbm, w_hbm, pre_hbm, gh_hbm, gi_ref, gwb,
    xall, gall, pre, gh, w, part, psib, r1, r2, r3, r4, own, onward,
    ag_s, ag_r, sib_s, sib_r, g_s, g_r, ps_s, ps_r, rs_s, rs_r, local,
):
    dep, row, x = lax.axis_index("depth"), lax.axis_index("row"), lax.axis_index("col")
    z_lo, core = dep // 2, dep % 2
    y, z = row // 2, (row % 2) * 2 + z_lo
    place = {"x": x, "y": y, "z": z}

    def device(x, y, z, core):
        return ((z % 2) * 2 + core, y * 2 + z // 2, x)

    def towards(axis, step):
        there = dict(place)
        there[axis] = (place[axis] + step) % N
        return device(there["x"], there["y"], there["z"], core)

    sibling = device(x, y, z, 1 - core)

    ag_s, ag_r = Slots(ag_s, 64), Slots(ag_r, AG_SEMS)
    sib_s, sib_r = Slots(sib_s, SIB_SEMS), Slots(sib_r, SIB_SEMS)
    g_s, g_r = Slots(g_s, G_SEMS), Slots(g_r, G_SEMS)
    ps_s, ps_r = Slots(ps_s, PS_SEMS), Slots(ps_r, PS_SEMS)
    rs_s, rs_r = Slots(rs_s, RS_SEMS), Slots(rs_r, RS_SEMS)
    local = Slots(local, LOCAL_SEMS)

    barrier = pltpu.get_barrier_semaphore()
    neighbours = [sibling] + [towards(axis, step) for axis in "xyz" for step in (1, -1)]
    for there in neighbours:
        pl.semaphore_signal(barrier, inc=1, device_id=there, device_id_type=MESH)

    own_row = pl.multiple_of((dep * 8 + row) * TOK, 16)
    loads = {
        "pre": pltpu.make_async_copy(pre_hbm, pre, local["pre"]),
        "gh": pltpu.make_async_copy(gh_hbm, gh, local["gh"]),
        "x0": pltpu.make_async_copy(x_hbm.at[:, pl.ds(0, HALF)], xall.at[0, pl.ds(own_row, TOK)], local["x0"]),
        "x1": pltpu.make_async_copy(x_hbm.at[:, pl.ds(HALF, HALF)], xall.at[1, pl.ds(own_row, TOK)], local["x1"]),
        "w": pltpu.make_async_copy(w_hbm, w, local["w"]),
    }
    for name in ("x0", "x1", "pre", "gh", "w"):
        loads[name].start()

    pending = []

    def send(src, dst, s, r, there):
        copy = pltpu.make_async_remote_copy(
            src_ref=src, dst_ref=dst, send_sem=s, recv_sem=r, device_id=there, device_id_type=MESH
        )
        copy.start()
        return copy

    def arrived(dst, s, r):
        pltpu.make_async_remote_copy(
            src_ref=dst, dst_ref=dst, send_sem=s, recv_sem=r, device_id=sibling, device_id_type=MESH
        ).wait_recv()

    def drain():
        while pending:
            pending.pop(0).wait_send()

    axes = (("y", "z"), ("z", "y"))

    def x_rows(h, o1, o2, of_core):
        first, second = (place[axes[h][0]] + o1) % N, (place[axes[h][1]] + o2) % N
        yy, zz = (first, second) if h == 0 else (second, first)
        return pl.multiple_of((((zz % 2) * 2 + of_core) * 8 + yy * 2 + zz // 2) * TOK, 16)

    def x_block(h, o1, o2, sub, of_core):
        rows = pl.ds(x_rows(h, o1, o2, of_core), TOK)
        if sub is None:
            return xall.at[h, rows]
        return xall.at[h, rows, pl.ds(sub * SUB, SUB)]

    def x_send(h, o1, o2, sub, along, step):
        block = x_block(h, o1, o2, sub, core)
        there = ((o1 - step) % N, o2) if along == 0 else (o1, (o2 - step) % N)
        pending.append(
            send(block, block, ag_s[h, o1, o2, sub, along, step], ag_r[(h, *there, sub)], towards(axes[h][along], step))
        )

    def x_arrived(h, o1, o2, sub):
        arrived(x_block(h, o1, o2, sub, core), ag_s[h, 0, 0, None, 0, 1], ag_r[h, o1, o2, sub])

    def x_share(h, o1, o2):
        block = x_block(h, o1, o2, None, core)
        pending.append(send(block, block, sib_s[h, o1, o2], sib_r[h, o1, o2], sibling))

    def x_shared(h, o1, o2):
        arrived(x_block(h, o1, o2, None, 1 - core), sib_s[h, 0, 0], sib_r[h, o1, o2])

    def x_first(h, o1):
        x_arrived(h, o1, 0, None)
        x_send(h, o1, 0, 0 if o1 == 3 else 1, 0, 1 if o1 == 3 else -1)

    def x_turn(h, o1):
        for step in (1, -1):
            x_send(h, o1, 0, None, 1, step)
        x_share(h, o1, 0)

    def x_far(h):
        for sub in (0, 1):
            x_arrived(h, 2, 0, sub)
            x_send(h, 2, 0, sub, 1, 1)
            x_send(h, 2, 0, sub, 1, -1)
        x_share(h, 2, 0)

    def x_second(h, o1):
        if o1 == 2:
            for o2, sub in ((3, 0), (1, 1)):
                x_arrived(h, 2, o2, sub)
                x_send(h, 2, o2, sub, 1, 1 if o2 == 3 else -1)
            for o2, sub in ((3, 1), (1, 0)):
                x_arrived(h, 2, o2, sub)
                x_share(h, 2, o2)
            return
        for o2 in (3, 1):
            x_arrived(h, o1, o2, None)
            x_send(h, o1, o2, 0 if o2 == 3 else 1, 1, 1 if o2 == 3 else -1)
            x_share(h, o1, o2)

    def x_last(h, o1):
        for sub in (0, 1):
            x_arrived(h, o1, 2, sub)
        x_share(h, o1, 2)

    def g_block(o, q):
        return gall.at[pl.ds(pl.multiple_of(((x + o) % N) * BLOCK + q * CHUNK, 16), CHUNK)]

    def g_send(o, q, step):
        block = g_block(o, q)
        pending.append(send(block, block, g_s[o, q, step], g_r[(o - step) % N, q], towards("x", step)))

    def g_arrived(o, q):
        arrived(g_block(o, q), g_s[0, 0, 1], g_r[o, q])

    def g_forward(o, q):
        g_arrived(o, q)
        g_send(o, q, 1 if o == 3 else -1)

    def g_compute(q):
        @pl.loop(0, CHUNK // 32)
        def _(i):
            rows = pl.ds(pl.multiple_of(q * CHUNK + i * 32, 32), 32)
            slope = gelu_slope(pre[rows].astype(F32))
            value = (gh[rows].astype(F32) * slope).astype(BF)
            gall[pl.ds(pl.multiple_of(x * BLOCK + q * CHUNK + i * 32, 32), 32)] = value

    def partial(o, h):
        block = (x + o) % N
        away, z_of = (block + core) % 2, block // 2
        rows = pl.ds(pl.multiple_of(block * BLOCK, 16), BLOCK)
        @pl.loop(0, 2)
        def _(n):
            product = lax.dot_general(
                gall[rows],
                w[pl.ds(pl.multiple_of(h * HALF + n * SUB, SUB), SUB)],
                (((1,), (1,)), ((), ())),
                preferred_element_type=F32,
            )
            part[away, z_of, h, :, pl.ds(pl.multiple_of(n * SUB, SUB), SUB)] = product.astype(BF)

        @pl.when(away == 1)
        def _():
            for yy in range(N):
                piece = pl.ds(yy * CHUNK, CHUNK)
                slot = (o // 2 * 2 + h) * N + yy
                send(
                    part.at[1, z_of, h, piece], psib.at[z_of, h, piece],
                    ps_s.ref.at[slot], ps_r.ref.at[(z_of * 2 + h) * N + yy], sibling,
                )

    def sib_part(zl, h, yy):
        piece = psib.at[zl, h, pl.ds(pl.multiple_of(yy * CHUNK, 16), CHUNK)]
        arrived(piece, ps_s.ref.at[0], ps_r.ref.at[(zl * 2 + h) * N + yy])

    rs_axes = (("z", "y"), ("y", "z"))

    def target(h, oa, ob):
        a, b = (place[rs_axes[h][0]] + oa) % N, (place[rs_axes[h][1]] + ob) % N
        zz, yy = (a, b) if h == 0 else (b, a)
        return zz % 2, pl.multiple_of(yy * CHUNK + (zz // 2) * TOK, 16), yy

    def rows16(body):
        @pl.loop(0, TOK // 16)
        def _(i):
            body(pl.multiple_of(i * 16, 16))

    def whole(h, zl, row0, i):
        at = pl.ds(pl.multiple_of(row0 + i, 16), 16)
        return part[0, zl, h, at].astype(F32) + psib[zl, h, at].astype(F32)

    def first_step(h, ob):
        zl, row0, yy = target(h, 2, ob)
        if h == 0 or ob in (2, 1):
            sib_part(zl, h, yy)

        def add(i):
            part[0, zl, h, pl.ds(pl.multiple_of(row0 + i, 16), 16)] = whole(h, zl, row0, i).astype(BF)

        rows16(add)
        for sub, step in ((0, 1), (1, -1)):
            pending.append(send(
                part.at[0, zl, h, pl.ds(row0, TOK), pl.ds(sub * SUB, SUB)], r1.at[h, sub, ob],
                rs_s[1, h, sub, ob], rs_r[1, h, sub, ob], towards(rs_axes[h][0], step),
            ))

    def second_step(h, ob):
        for sub, oa, step in ((0, 1, 1), (1, 3, -1)):
            zl, row0, yy = target(h, oa, ob)
            if (h == 0 and sub == 0) or (h == 1 and ob in (2, 1)):
                sib_part(zl, h, yy)
            arrived(r1.at[h, sub, ob], rs_s[1, h, sub, ob], rs_r[1, h, sub, ob])
            got, kept = pl.ds(sub * SUB, SUB), pl.ds((1 - sub) * SUB, SUB)

            def add(i):
                at = pl.ds(pl.multiple_of(row0 + i, 16), 16)
                part[0, zl, h, at, got] = (
                    part[0, zl, h, at, got].astype(F32) + psib[zl, h, at, got].astype(F32)
                    + r1[h, sub, ob, pl.ds(i, 16)].astype(F32)
                ).astype(BF)
                part[0, zl, h, at, kept] = (
                    part[0, zl, h, at, kept].astype(F32) + psib[zl, h, at, kept].astype(F32)
                ).astype(BF)

            rows16(add)
            pending.append(send(
                part.at[0, zl, h, pl.ds(row0, TOK)], r2.at[h, sub, ob],
                rs_s[2, h, sub, ob], rs_r[2, h, sub, ob], towards(rs_axes[h][0], step),
            ))

    def third_step(h, ob):
        zl, row0, yy = target(h, 0, ob)
        if h == 1 and ob in (2, 1):
            sib_part(zl, h, yy)
        for sub in (0, 1):
            arrived(r2.at[h, sub, ob], rs_s[2, h, sub, ob], rs_r[2, h, sub, ob])

        def add(i):
            at, here = pl.ds(i, 16), pl.ds(pl.multiple_of(row0 + i, 16), 16)
            total = whole(h, zl, row0, i) + r2[h, 0, ob, at].astype(F32) + r2[h, 1, ob, at].astype(F32)
            if ob == 0:
                own[h, at] = total
            elif ob == 2:
                part[0, zl, h, here] = total.astype(BF)
            else:
                sub = 0 if ob == 1 else 1
                onward[h, sub, at] = total[:, sub * SUB:(sub + 1) * SUB]
                part[0, zl, h, here, pl.ds((1 - sub) * SUB, SUB)] = (
                    total[:, (1 - sub) * SUB:(2 - sub) * SUB].astype(BF)
                )

        rows16(add)

    def fourth_step(h):
        zl, row0, _ = target(h, 0, 2)
        for sub, step in ((0, 1), (1, -1)):
            pending.append(send(
                part.at[0, zl, h, pl.ds(row0, TOK), pl.ds(sub * SUB, SUB)], r3.at[h, sub],
                rs_s[3, h, sub], rs_r[3, h, sub], towards(rs_axes[h][1], step),
            ))

    def fifth_step_early(h, sub):
        ob, step = ((1, 1), (3, -1))[sub]
        zl, row0, _ = target(h, 0, ob)
        kept = pl.ds((1 - sub) * SUB, SUB)
        pending.append(send(
            part.at[0, zl, h, pl.ds(row0, TOK), kept], r4.at[h, sub, :, kept],
            rs_s[4, h, sub, 1], rs_r[4, h, sub, 1], towards(rs_axes[h][1], step),
        ))

    def fifth_step(h, sub):
        ob, step = ((1, 1), (3, -1))[sub]
        zl, row0, _ = target(h, 0, ob)
        got = pl.ds(sub * SUB, SUB)
        arrived(r3.at[h, sub], rs_s[3, h, sub], rs_r[3, h, sub])

        def add(i):
            at = pl.ds(i, 16)
            part[0, zl, h, pl.ds(pl.multiple_of(row0 + i, 16), 16), got] = (
                onward[h, sub, at] + r3[h, sub, at].astype(F32)
            ).astype(BF)

        rows16(add)
        pending.append(send(
            part.at[0, zl, h, pl.ds(row0, TOK), got], r4.at[h, sub, :, got],
            rs_s[4, h, sub, 0], rs_r[4, h, sub, 0], towards(rs_axes[h][1], step),
        ))

    def sixth_step(h):
        for sub in (0, 1):
            for late in (1, 0):
                cols = pl.ds((sub if late == 0 else 1 - sub) * SUB, SUB)
                arrived(r4.at[h, sub, :, cols], rs_s[4, h, sub, late], rs_r[4, h, sub, late])

        def add(i):
            at = pl.ds(i, 16)
            gi_ref[at, pl.ds(h * HALF, HALF)] = (
                own[h, at] + r4[h, 0, at].astype(F32) + r4[h, 1, at].astype(F32)
            ).astype(BF)

        rows16(add)

    tiles = HALF // GTILE

    def weight_tile(n):
        h, m = n // tiles, n % tiles
        product = lax.dot_general(
            xall[h, :, pl.ds(m * GTILE, GTILE)], gall[...], (((0,), (0,)), ((), ())), preferred_element_type=F32
        )
        rows = pl.ds(n * GTILE, GTILE)
        gwb[rows] = product.astype(BF)

    both = (0, 1)
    loads["pre"].wait()
    loads["gh"].wait()
    for q in range(4):
        g_compute(q)
    loads["x0"].wait()
    loads["x1"].wait()
    pl.semaphore_wait(barrier, len(neighbours))
    for along in (0, 1):
        for h in both:
            for step in (1, -1):
                x_send(h, 0, 0, None, along, step)
    for q in (0, 2, 1, 3):
        g_send(0, q, 1)
        g_send(0, q, -1)
    for h in both:
        x_share(h, 0, 0)
    loads["w"].wait()
    for h in both:
        partial(0, h)
    for o in (3, 1):
        for h in both:
            x_first(h, o)
    for o in (3, 1):
        for h in both:
            x_turn(h, o)
    g_forward(3, 0)
    g_forward(1, 2)
    for h in both:
        x_second(h, 0)
    g_forward(3, 1)
    g_forward(1, 3)
    for h in both:
        x_far(h)
    for h in both:
        x_second(h, 3)
    for q in (2, 3):
        g_arrived(3, q)
    partial(3, 0)
    for h in both:
        x_second(h, 1)
    partial(3, 1)
    for q in (0, 1):
        g_arrived(1, q)
    partial(1, 0)
    for h in both:
        x_last(h, 0)
    partial(1, 1)
    for h in both:
        x_second(h, 2)
    for q in range(4):
        g_arrived(2, q)
    for h in both:
        partial(2, h)
    for h in both:
        for ob in (2, 1, 3, 0):
            first_step(h, ob)
    for ob in (2, 1, 3):
        for h in both:
            second_step(h, ob)
    for o1 in (3, 1, 2):
        for h in both:
            x_last(h, o1)
    for o1 in range(N):
        for o2 in range(N):
            for h in both:
                x_shared(h, o1, o2)
    weight_tile(0)
    weight_tile(1)
    for h in both:
        third_step(h, 2)
        fourth_step(h)
    for h in both:
        second_step(h, 0)
    weight_tile(2)
    weight_tile(3)
    for h in both:
        third_step(h, 1)
        fifth_step_early(h, 0)
    weight_tile(4)
    for h in both:
        third_step(h, 3)
        fifth_step_early(h, 1)
    weight_tile(5)
    for slot in range(PS_SEMS):
        piece = part.at[1, 0, 0, pl.ds(0, CHUNK)]
        pltpu.make_async_remote_copy(
            src_ref=piece, dst_ref=piece, send_sem=ps_s.ref.at[slot], recv_sem=ps_r.ref.at[0],
            device_id=sibling, device_id_type=MESH,
        ).wait_send()
    for h in both:
        for sub in (0, 1):
            fifth_step(h, sub)
    while len(pending) > 32:
        pending.pop(0).wait_send()
    for h in both:
        third_step(h, 0)
    for h in both:
        sixth_step(h)
    drain()


def write_out(gi, gw, gi_hbm, gw_hbm, sems):
    rows = FEAT // WRITES
    copies = [pltpu.make_async_copy(gi, gi_hbm, sems.at[WRITES])]
    for n in range(WRITES):
        part = pl.ds(n * rows, rows)
        copies.append(pltpu.make_async_copy(gw.at[part], gw_hbm.at[part], sems.at[n]))
    for copy in copies:
        copy.start()
    for copy in copies:
        copy.wait()


def per_device(inputs, weight, pre_act, grad_hidden):
    dma = pltpu.SemaphoreType.DMA
    grads = pl.pallas_call(
        kernel,
        out_shape=(pltpu.VMEM((TOK, FEAT), BF), pltpu.VMEM((FEAT, HID), BF)),
        in_specs=[pl.BlockSpec(memory_space=pl.ANY)] * 4,
        out_specs=(pl.BlockSpec(memory_space=pltpu.VMEM), pl.BlockSpec(memory_space=pltpu.VMEM)),
        scratch_shapes=[
            pltpu.VMEM((2, N * BLOCK, HALF), BF),
            pltpu.VMEM((N * BLOCK, HID), BF),
            pltpu.VMEM((BLOCK, HID), BF),
            pltpu.VMEM((BLOCK, HID), BF),
            pltpu.VMEM((FEAT, HID), BF),
            pltpu.VMEM((2, 2, 2, BLOCK, HALF), BF),
            pltpu.VMEM((2, 2, BLOCK, HALF), BF),
            pltpu.VMEM((2, 2, N, TOK, SUB), BF),
            pltpu.VMEM((2, 2, N, TOK, HALF), BF),
            pltpu.VMEM((2, 2, TOK, SUB), BF),
            pltpu.VMEM((2, 2, TOK, HALF), BF),
            pltpu.VMEM((2, TOK, HALF), F32),
            pltpu.VMEM((2, 2, TOK, SUB), F32),
            dma((64,)), dma((AG_SEMS,)),
            dma((SIB_SEMS,)), dma((SIB_SEMS,)),
            dma((G_SEMS,)), dma((G_SEMS,)),
            dma((PS_SEMS,)), dma((PS_SEMS,)),
            dma((RS_SEMS,)), dma((RS_SEMS,)),
            dma((LOCAL_SEMS,)),
        ],
        compiler_params=pltpu.CompilerParams(
            collective_id=0, has_side_effects=True, vmem_limit_bytes=50 << 20
        ),
        cost_estimate=pl.CostEstimate(flops=14_500_000_000, bytes_accessed=16_000_000, transcendentals=300_000),
        name="gelu_up_backward",
    )(inputs, weight, pre_act, grad_hidden)
    return pl.pallas_call(
        write_out,
        out_shape=tuple(jax.ShapeDtypeStruct(g.shape, g.dtype) for g in grads),
        in_specs=[pl.BlockSpec(memory_space=pltpu.VMEM)] * 2,
        out_specs=[pl.BlockSpec(memory_space=pl.ANY)] * 2,
        scratch_shapes=[dma((1 + WRITES,))],
        compiler_params=pltpu.CompilerParams(vmem_limit_bytes=1 << 20),
        name="write_out",
    )(*(pltpu.with_memory_space_constraint(g, pltpu.VMEM) for g in grads))


def solution(mesh):
    return jax.shard_map(
        per_device,
        mesh=mesh,
        in_specs=(
            P(("depth", "row"), "col"),
            P("col", ("depth", "row")),
            P("col", ("depth", "row")),
            P("col", ("depth", "row")),
        ),
        out_specs=(P(("depth", "row"), "col"), P("col", ("depth", "row"))),
        check_vma=False,
    )
```

```python
import functools
import math

import jax
import jax.numpy as jnp
from jax import lax
from jax.experimental import pallas as pl
from jax.experimental.pallas import tpu as pltpu
from jax.sharding import PartitionSpec as P

MESH = pl.DeviceIdType.MESH
BF, F32 = jnp.bfloat16, jnp.float32

N = 4
TOK = 48
HALF = 1536
SUB = HALF // 2
FEAT = 2 * HALF
HID = 768
BLOCK = 384
CHUNK = 96
GTILE = 512
WRITES = 4


def gelu_slope(pre):
    coeff = math.sqrt(2.0 / math.pi)
    inner = coeff * (pre + 0.044715 * pre * pre * pre)
    tanh_val = jnp.tanh(inner)
    return 0.5 * (1.0 + tanh_val) + 0.5 * pre * (1.0 - tanh_val * tanh_val) * coeff * (
        1.0 + 3.0 * 0.044715 * pre * pre
    )


class Slots:
    def __init__(self, ref, size):
        self.ref, self.size, self.keys = ref, size, {}

    def __getitem__(self, key):
        place = self.keys.setdefault(key, len(self.keys))
        assert place < self.size
        return self.ref.at[place]


AG_SEMS, SIB_SEMS, G_SEMS, PS_SEMS, RS_SEMS, LOCAL_SEMS = 44, 32, 12, 16, 44, 16


def kernel(
    x_hbm, w_hbm, pre_hbm, gh_hbm, gi_ref, gwb,
    xall, gall, pre, gh, w, part, psib, r1, r2, r3, r4, own, onward,
    ag_s, ag_r, sib_s, sib_r, g_s, g_r, ps_s, ps_r, rs_s, rs_r, local,
):
    dep, row, x = lax.axis_index("depth"), lax.axis_index("row"), lax.axis_index("col")
    z_lo, core = dep // 2, dep % 2
    y, z = row // 2, (row % 2) * 2 + z_lo
    place = {"x": x, "y": y, "z": z}

    def device(x, y, z, core):
        return ((z % 2) * 2 + core, y * 2 + z // 2, x)

    def towards(axis, step):
        there = dict(place)
        there[axis] = (place[axis] + step) % N
        return device(there["x"], there["y"], there["z"], core)

    sibling = device(x, y, z, 1 - core)

    ag_s, ag_r = Slots(ag_s, 64), Slots(ag_r, AG_SEMS)
    sib_s, sib_r = Slots(sib_s, SIB_SEMS), Slots(sib_r, SIB_SEMS)
    g_s, g_r = Slots(g_s, G_SEMS), Slots(g_r, G_SEMS)
    ps_s, ps_r = Slots(ps_s, PS_SEMS), Slots(ps_r, PS_SEMS)
    rs_s, rs_r = Slots(rs_s, RS_SEMS), Slots(rs_r, RS_SEMS)
    local = Slots(local, LOCAL_SEMS)

    barrier = pltpu.get_barrier_semaphore()
    neighbours = [sibling] + [towards(axis, step) for axis in "xyz" for step in (1, -1)]
    for there in neighbours:
        pl.semaphore_signal(barrier, inc=1, device_id=there, device_id_type=MESH)

    own_row = pl.multiple_of((dep * 8 + row) * TOK, 16)
    loads = {
        "pre": pltpu.make_async_copy(pre_hbm, pre, local["pre"]),
        "gh": pltpu.make_async_copy(gh_hbm, gh, local["gh"]),
        "x0": pltpu.make_async_copy(x_hbm.at[:, pl.ds(0, HALF)], xall.at[0, pl.ds(own_row, TOK)], local["x0"]),
        "x1": pltpu.make_async_copy(x_hbm.at[:, pl.ds(HALF, HALF)], xall.at[1, pl.ds(own_row, TOK)], local["x1"]),
        "w": pltpu.make_async_copy(w_hbm, w, local["w"]),
    }
    for name in ("x0", "x1", "pre", "gh", "w"):
        loads[name].start()

    pending = []

    def send(src, dst, s, r, there):
        copy = pltpu.make_async_remote_copy(
            src_ref=src, dst_ref=dst, send_sem=s, recv_sem=r, device_id=there, device_id_type=MESH
        )
        copy.start()
        return copy

    def arrived(dst, s, r):
        pltpu.make_async_remote_copy(
            src_ref=dst, dst_ref=dst, send_sem=s, recv_sem=r, device_id=sibling, device_id_type=MESH
        ).wait_recv()

    def drain(left):
        while len(pending) > left:
            pending.pop(0).wait_send()

    axes = (("y", "z"), ("z", "y"))

    def x_rows(h, o1, o2, of_core):
        first, second = (place[axes[h][0]] + o1) % N, (place[axes[h][1]] + o2) % N
        yy, zz = (first, second) if h == 0 else (second, first)
        return pl.multiple_of((((zz % 2) * 2 + of_core) * 8 + yy * 2 + zz // 2) * TOK, 16)

    def x_block(h, o1, o2, sub, of_core):
        rows = pl.ds(x_rows(h, o1, o2, of_core), TOK)
        if sub is None:
            return xall.at[h, rows]
        return xall.at[h, rows, pl.ds(sub * SUB, SUB)]

    def x_send(h, o1, o2, sub, along, step):
        block = x_block(h, o1, o2, sub, core)
        there = ((o1 - step) % N, o2) if along == 0 else (o1, (o2 - step) % N)
        pending.append(
            send(block, block, ag_s[h, o1, o2, sub, along, step], ag_r[(h, *there, sub)], towards(axes[h][along], step))
        )

    def x_send_own(h, along, step):
        there = (-step % N, 0) if along == 0 else (0, -step % N)
        pending.append(send(
            x_hbm.at[:, pl.ds(h * HALF, HALF)], x_block(h, 0, 0, None, core),
            ag_s[h, 0, 0, None, along, step], ag_r[(h, *there, None)], towards(axes[h][along], step),
        ))

    def x_arrived(h, o1, o2, sub):
        arrived(x_block(h, o1, o2, sub, core), ag_s[h, 0, 0, None, 0, 1], ag_r[h, o1, o2, sub])

    def x_share(h, o1, o2):
        block = x_block(h, o1, o2, None, core)
        pending.append(send(block, block, sib_s[h, o1, o2], sib_r[h, o1, o2], sibling))

    def x_shared(h, o1, o2):
        arrived(x_block(h, o1, o2, None, 1 - core), sib_s[h, 0, 0], sib_r[h, o1, o2])

    def x_first(h, o1):
        x_arrived(h, o1, 0, None)
        x_send(h, o1, 0, 0 if o1 == 3 else 1, 0, 1 if o1 == 3 else -1)

    def x_turn(h, o1):
        for step in (1, -1):
            x_send(h, o1, 0, None, 1, step)
        x_share(h, o1, 0)

    def x_far(h):
        for sub in (0, 1):
            x_arrived(h, 2, 0, sub)
            x_send(h, 2, 0, sub, 1, 1)
            x_send(h, 2, 0, sub, 1, -1)
        x_share(h, 2, 0)

    def x_second(h, o1):
        if o1 == 2:
            for o2, sub in ((3, 0), (1, 1)):
                x_arrived(h, 2, o2, sub)
                x_send(h, 2, o2, sub, 1, 1 if o2 == 3 else -1)
            for o2, sub in ((3, 1), (1, 0)):
                x_arrived(h, 2, o2, sub)
                x_share(h, 2, o2)
            return
        for o2 in (3, 1):
            x_arrived(h, o1, o2, None)
            x_send(h, o1, o2, 0 if o2 == 3 else 1, 1, 1 if o2 == 3 else -1)
            x_share(h, o1, o2)

    def x_last(h, o1):
        for sub in (0, 1):
            x_arrived(h, o1, 2, sub)
        x_share(h, o1, 2)

    def g_block(o, q):
        return gall.at[pl.ds(pl.multiple_of(((x + o) % N) * BLOCK + q * CHUNK, 16), CHUNK)]

    def g_send(o, q, step):
        block = g_block(o, q)
        pending.append(send(block, block, g_s[o, q, step], g_r[(o - step) % N, q], towards("x", step)))

    def g_arrived(o, q):
        arrived(g_block(o, q), g_s[0, 0, 1], g_r[o, q])

    def g_forward(o, q):
        g_arrived(o, q)
        g_send(o, q, 1 if o == 3 else -1)

    def g_compute(q):
        @pl.loop(0, CHUNK // 32)
        def _(i):
            rows = pl.ds(pl.multiple_of(q * CHUNK + i * 32, 32), 32)
            slope = gelu_slope(pre[rows].astype(F32))
            value = (gh[rows].astype(F32) * slope).astype(BF)
            gall[pl.ds(pl.multiple_of(x * BLOCK + q * CHUNK + i * 32, 32), 32)] = value

    def partial(o, h):
        block = (x + o) % N
        away, z_of = (block + core) % 2, block // 2
        rows = pl.ds(pl.multiple_of(block * BLOCK, 16), BLOCK)
        @pl.loop(0, 2)
        def _(n):
            product = lax.dot_general(
                gall[rows],
                w[pl.ds(pl.multiple_of(h * HALF + n * SUB, SUB), SUB)],
                (((1,), (1,)), ((), ())),
                preferred_element_type=F32,
            )
            part[away, z_of, h, :, pl.ds(pl.multiple_of(n * SUB, SUB), SUB)] = product.astype(BF)

        @pl.when(away == 1)
        def _():
            for yy in range(N):
                piece = pl.ds(yy * CHUNK, CHUNK)
                slot = (o // 2 * 2 + h) * N + yy
                send(
                    part.at[1, z_of, h, piece], psib.at[z_of, h, piece],
                    ps_s.ref.at[slot], ps_r.ref.at[(z_of * 2 + h) * N + yy], sibling,
                )

    def sib_part(zl, h, yy):
        piece = psib.at[zl, h, pl.ds(pl.multiple_of(yy * CHUNK, 16), CHUNK)]
        arrived(piece, ps_s.ref.at[0], ps_r.ref.at[(zl * 2 + h) * N + yy])

    rs_axes = (("z", "y"), ("y", "z"))

    def target(h, oa, ob):
        a, b = (place[rs_axes[h][0]] + oa) % N, (place[rs_axes[h][1]] + ob) % N
        zz, yy = (a, b) if h == 0 else (b, a)
        return zz % 2, pl.multiple_of(yy * CHUNK + (zz // 2) * TOK, 16), yy

    def rows16(body):
        @pl.loop(0, TOK // 16)
        def _(i):
            body(pl.multiple_of(i * 16, 16))

    def whole(h, zl, row0, i):
        at = pl.ds(pl.multiple_of(row0 + i, 16), 16)
        return part[0, zl, h, at].astype(F32) + psib[zl, h, at].astype(F32)

    def first_step(h, ob):
        zl, row0, yy = target(h, 2, ob)
        if h == 0 or ob in (2, 1):
            sib_part(zl, h, yy)

        def add(i):
            part[0, zl, h, pl.ds(pl.multiple_of(row0 + i, 16), 16)] = whole(h, zl, row0, i).astype(BF)

        rows16(add)
        for sub, step in ((0, 1), (1, -1)):
            send(
                part.at[0, zl, h, pl.ds(row0, TOK), pl.ds(sub * SUB, SUB)], r1.at[h, sub, ob],
                rs_s[1, h, sub, ob], rs_r[1, h, sub, ob], towards(rs_axes[h][0], step),
            )

    def first_sent(h, ob):
        zl, row0, _ = target(h, 2, ob)
        for sub, step in ((0, 1), (1, -1)):
            pending.append(pltpu.make_async_remote_copy(
                src_ref=part.at[0, zl, h, pl.ds(row0, TOK), pl.ds(sub * SUB, SUB)], dst_ref=r1.at[h, sub, ob],
                send_sem=rs_s[1, h, sub, ob], recv_sem=rs_r[1, h, sub, ob],
                device_id=towards(rs_axes[h][0], step), device_id_type=MESH,
            ))

    def second_step(h, ob):
        for sub, oa, step in ((0, 1, 1), (1, 3, -1)):
            zl, row0, yy = target(h, oa, ob)
            if (h == 0 and sub == 0) or (h == 1 and ob in (2, 1)):
                sib_part(zl, h, yy)
            arrived(r1.at[h, sub, ob], rs_s[1, h, sub, ob], rs_r[1, h, sub, ob])
            got, kept = pl.ds(sub * SUB, SUB), pl.ds((1 - sub) * SUB, SUB)

            def add(i):
                at = pl.ds(pl.multiple_of(row0 + i, 16), 16)
                part[0, zl, h, at, got] = (
                    part[0, zl, h, at, got].astype(F32) + psib[zl, h, at, got].astype(F32)
                    + r1[h, sub, ob, pl.ds(i, 16)].astype(F32)
                ).astype(BF)
                part[0, zl, h, at, kept] = (
                    part[0, zl, h, at, kept].astype(F32) + psib[zl, h, at, kept].astype(F32)
                ).astype(BF)

            rows16(add)
            pending.append(send(
                part.at[0, zl, h, pl.ds(row0, TOK)], r2.at[h, sub, ob],
                rs_s[2, h, sub, ob], rs_r[2, h, sub, ob], towards(rs_axes[h][0], step),
            ))

    def third_step(h, ob):
        zl, row0, yy = target(h, 0, ob)
        if h == 1 and ob in (2, 1):
            sib_part(zl, h, yy)
        for sub in (0, 1):
            arrived(r2.at[h, sub, ob], rs_s[2, h, sub, ob], rs_r[2, h, sub, ob])

        def add(i):
            at, here = pl.ds(i, 16), pl.ds(pl.multiple_of(row0 + i, 16), 16)
            total = whole(h, zl, row0, i) + r2[h, 0, ob, at].astype(F32) + r2[h, 1, ob, at].astype(F32)
            if ob == 0:
                own[h, at] = total
            elif ob == 2:
                part[0, zl, h, here] = total.astype(BF)
            else:
                sub = 0 if ob == 1 else 1
                onward[h, sub, at] = total[:, sub * SUB:(sub + 1) * SUB]
                part[0, zl, h, here, pl.ds((1 - sub) * SUB, SUB)] = (
                    total[:, (1 - sub) * SUB:(2 - sub) * SUB].astype(BF)
                )

        rows16(add)

    def fourth_step(h):
        zl, row0, _ = target(h, 0, 2)
        for sub, step in ((0, 1), (1, -1)):
            pending.append(send(
                part.at[0, zl, h, pl.ds(row0, TOK), pl.ds(sub * SUB, SUB)], r3.at[h, sub],
                rs_s[3, h, sub], rs_r[3, h, sub], towards(rs_axes[h][1], step),
            ))

    def fifth_step_early(h, sub):
        ob, step = ((1, 1), (3, -1))[sub]
        zl, row0, _ = target(h, 0, ob)
        kept = pl.ds((1 - sub) * SUB, SUB)
        pending.append(send(
            part.at[0, zl, h, pl.ds(row0, TOK), kept], r4.at[h, sub, :, kept],
            rs_s[4, h, sub, 1], rs_r[4, h, sub, 1], towards(rs_axes[h][1], step),
        ))

    def fifth_step(h, sub):
        ob, step = ((1, 1), (3, -1))[sub]
        zl, row0, _ = target(h, 0, ob)
        got = pl.ds(sub * SUB, SUB)
        arrived(r3.at[h, sub], rs_s[3, h, sub], rs_r[3, h, sub])

        def add(i):
            at = pl.ds(i, 16)
            part[0, zl, h, pl.ds(pl.multiple_of(row0 + i, 16), 16), got] = (
                onward[h, sub, at] + r3[h, sub, at].astype(F32)
            ).astype(BF)

        rows16(add)
        pending.append(send(
            part.at[0, zl, h, pl.ds(row0, TOK), got], r4.at[h, sub, :, got],
            rs_s[4, h, sub, 0], rs_r[4, h, sub, 0], towards(rs_axes[h][1], step),
        ))

    def sixth_step_early(h):
        for sub in (0, 1):
            kept = pl.ds((1 - sub) * SUB, SUB)
            arrived(r4.at[h, sub, :, kept], rs_s[4, h, sub, 1], rs_r[4, h, sub, 1])

            def add(i):
                at = pl.ds(i, 16)
                own[h, at, kept] = own[h, at, kept] + r4[h, sub, at, kept].astype(F32)

            rows16(add)

    def sixth_step(h, sub):
        got = pl.ds(sub * SUB, SUB)
        arrived(r4.at[h, sub, :, got], rs_s[4, h, sub, 0], rs_r[4, h, sub, 0])

        def add(i):
            at = pl.ds(i, 16)
            gi_ref[at, pl.ds(h * HALF + sub * SUB, SUB)] = (
                own[h, at, got] + r4[h, sub, at, got].astype(F32)
            ).astype(BF)

        rows16(add)

    tiles = HALF // GTILE

    def weight_tile(n):
        h, m = n // tiles, n % tiles
        product = lax.dot_general(
            xall[h, :, pl.ds(m * GTILE, GTILE)], gall[...], (((0,), (0,)), ((), ())), preferred_element_type=F32
        )
        rows = pl.ds(n * GTILE, GTILE)
        gwb[rows] = product.astype(BF)

    both = (0, 1)
    pl.semaphore_wait(barrier, len(neighbours))
    for along in (0, 1):
        for h in both:
            for step in (1, -1):
                x_send_own(h, along, step)
    loads["pre"].wait()
    loads["gh"].wait()
    for q in (0, 2, 1, 3):
        g_compute(q)
        g_send(0, q, 1)
        g_send(0, q, -1)
    loads["x0"].wait()
    loads["x1"].wait()
    for h in both:
        x_share(h, 0, 0)
    loads["w"].wait()
    for h in both:
        partial(0, h)
    for o in (3, 1):
        for h in both:
            x_first(h, o)
    for o in (3, 1):
        for h in both:
            x_turn(h, o)
    g_forward(3, 0)
    g_forward(1, 2)
    for h in both:
        x_second(h, 0)
    g_forward(3, 1)
    g_forward(1, 3)
    for h in both:
        x_far(h)
    for h in both:
        x_second(h, 3)
    for q in (2, 3):
        g_arrived(3, q)
    partial(3, 0)
    for h in both:
        x_second(h, 1)
    partial(3, 1)
    for q in (0, 1):
        g_arrived(1, q)
    partial(1, 0)
    for h in both:
        x_last(h, 0)
    partial(1, 1)
    early = (x + core) % 2 == 1

    def first_steps(halves):
        for h in halves:
            for ob in (2, 1, 3, 0):
                first_step(h, ob)

    def first_sends():
        for h in both:
            for ob in (2, 1, 3, 0):
                first_sent(h, ob)

    for h in both:
        x_second(h, 2)
    pl.when(early)(lambda: first_steps((0,)))
    for q in range(4):
        g_arrived(2, q)
    partial(2, 0)
    pl.when(early)(lambda: first_steps((1,)))
    partial(2, 1)
    pl.when(jnp.logical_not(early))(lambda: first_steps(both))
    first_sends()
    for ob in (2, 1, 3):
        for h in both:
            second_step(h, ob)
    for o1 in (3, 1, 2):
        for h in both:
            x_last(h, o1)
    for o1 in range(N):
        for o2 in range(N):
            for h in both:
                x_shared(h, o1, o2)
    weight_tile(0)
    weight_tile(1)
    for h in both:
        third_step(h, 2)
        fourth_step(h)
    for h in both:
        second_step(h, 0)
    weight_tile(2)
    weight_tile(3)
    for h in both:
        third_step(h, 1)
        fifth_step_early(h, 0)
    weight_tile(4)
    for h in both:
        third_step(h, 3)
        fifth_step_early(h, 1)
    weight_tile(5)
    for slot in range(PS_SEMS):
        piece = part.at[1, 0, 0, pl.ds(0, CHUNK)]
        pltpu.make_async_remote_copy(
            src_ref=piece, dst_ref=piece, send_sem=ps_s.ref.at[slot], recv_sem=ps_r.ref.at[0],
            device_id=sibling, device_id_type=MESH,
        ).wait_send()
    for h in both:
        for sub in (0, 1):
            fifth_step(h, sub)
    drain(12)
    for h in both:
        third_step(h, 0)
    for h in both:
        sixth_step_early(h)
    for sub in (0, 1):
        for h in both:
            sixth_step(h, sub)
    drain(0)


def write_out(gi, gw, gi_hbm, gw_hbm, sems):
    rows = FEAT // WRITES
    copies = [pltpu.make_async_copy(gi, gi_hbm, sems.at[WRITES])]
    for n in range(WRITES):
        part = pl.ds(n * rows, rows)
        copies.append(pltpu.make_async_copy(gw.at[part], gw_hbm.at[part], sems.at[n]))
    for copy in copies:
        copy.start()
    for copy in copies:
        copy.wait()


def per_device(inputs, weight, pre_act, grad_hidden):
    dma = pltpu.SemaphoreType.DMA
    grads = pl.pallas_call(
        kernel,
        out_shape=(pltpu.VMEM((TOK, FEAT), BF), pltpu.VMEM((FEAT, HID), BF)),
        in_specs=[pl.BlockSpec(memory_space=pl.ANY)] * 4,
        out_specs=(pl.BlockSpec(memory_space=pltpu.VMEM), pl.BlockSpec(memory_space=pltpu.VMEM)),
        scratch_shapes=[
            pltpu.VMEM((2, N * BLOCK, HALF), BF),
            pltpu.VMEM((N * BLOCK, HID), BF),
            pltpu.VMEM((BLOCK, HID), BF),
            pltpu.VMEM((BLOCK, HID), BF),
            pltpu.VMEM((FEAT, HID), BF),
            pltpu.VMEM((2, 2, 2, BLOCK, HALF), BF),
            pltpu.VMEM((2, 2, BLOCK, HALF), BF),
            pltpu.VMEM((2, 2, N, TOK, SUB), BF),
            pltpu.VMEM((2, 2, N, TOK, HALF), BF),
            pltpu.VMEM((2, 2, TOK, SUB), BF),
            pltpu.VMEM((2, 2, TOK, HALF), BF),
            pltpu.VMEM((2, TOK, HALF), F32),
            pltpu.VMEM((2, 2, TOK, SUB), F32),
            dma((64,)), dma((AG_SEMS,)),
            dma((SIB_SEMS,)), dma((SIB_SEMS,)),
            dma((G_SEMS,)), dma((G_SEMS,)),
            dma((PS_SEMS,)), dma((PS_SEMS,)),
            dma((RS_SEMS,)), dma((RS_SEMS,)),
            dma((LOCAL_SEMS,)),
        ],
        compiler_params=pltpu.CompilerParams(
            collective_id=0, has_side_effects=True, vmem_limit_bytes=50 << 20
        ),
        cost_estimate=pl.CostEstimate(flops=14_500_000_000, bytes_accessed=16_000_000, transcendentals=300_000),
        name="gelu_up_backward",
    )(inputs, weight, pre_act, grad_hidden)
    return pl.pallas_call(
        write_out,
        out_shape=tuple(jax.ShapeDtypeStruct(g.shape, g.dtype) for g in grads),
        in_specs=[pl.BlockSpec(memory_space=pltpu.VMEM)] * 2,
        out_specs=[pl.BlockSpec(memory_space=pl.ANY)] * 2,
        scratch_shapes=[dma((1 + WRITES,))],
        compiler_params=pltpu.CompilerParams(vmem_limit_bytes=1 << 20),
        name="write_out",
    )(*(pltpu.with_memory_space_constraint(g, pltpu.VMEM) for g in grads))


def solution(mesh):
    return jax.shard_map(
        per_device,
        mesh=mesh,
        in_specs=(
            P(("depth", "row"), "col"),
            P("col", ("depth", "row")),
            P("col", ("depth", "row")),
            P("col", ("depth", "row")),
        ),
        out_specs=(P(("depth", "row"), "col"), P("col", ("depth", "row"))),
        check_vma=False,
    )
```

```python
import functools
import math

import jax
import jax.numpy as jnp
from jax import lax
from jax.experimental import pallas as pl
from jax.experimental.pallas import tpu as pltpu
from jax.sharding import PartitionSpec as P

MESH = pl.DeviceIdType.MESH
BF, F32 = jnp.bfloat16, jnp.float32

N = 4
TOK = 48
HALF = 1536
SUB = HALF // 2
FEAT = 2 * HALF
HID = 768
BLOCK = 384
CHUNK = 96
GTILE = 512
WRITES = 4


def gelu_slope(pre):
    coeff = math.sqrt(2.0 / math.pi)
    inner = coeff * (pre + 0.044715 * pre * pre * pre)
    tanh_val = jnp.tanh(inner)
    return 0.5 * (1.0 + tanh_val) + 0.5 * pre * (1.0 - tanh_val * tanh_val) * coeff * (
        1.0 + 3.0 * 0.044715 * pre * pre
    )


class Slots:
    def __init__(self, ref, size):
        self.ref, self.size, self.keys = ref, size, {}

    def __getitem__(self, key):
        place = self.keys.setdefault(key, len(self.keys))
        assert place < self.size
        return self.ref.at[place]


AG_SEMS, SIB_SEMS, G_SEMS, PS_SEMS, RS_SEMS, LOCAL_SEMS = 44, 32, 12, 16, 44, 16


def kernel(
    x_hbm, w_hbm, pre_hbm, gh_hbm, gi_ref, gwb,
    xall, gall, pre, gh, w, part, psib, r1, r2, r3, r4, own, onward,
    ag_s, ag_r, sib_s, sib_r, g_s, g_r, ps_s, ps_r, rs_s, rs_r, local,
):
    dep, row, x = lax.axis_index("depth"), lax.axis_index("row"), lax.axis_index("col")
    z_lo, core = dep // 2, dep % 2
    y, z = row // 2, (row % 2) * 2 + z_lo
    place = {"x": x, "y": y, "z": z}

    def device(x, y, z, core):
        return ((z % 2) * 2 + core, y * 2 + z // 2, x)

    def towards(axis, step):
        there = dict(place)
        there[axis] = (place[axis] + step) % N
        return device(there["x"], there["y"], there["z"], core)

    sibling = device(x, y, z, 1 - core)

    ag_s, ag_r = Slots(ag_s, 64), Slots(ag_r, AG_SEMS)
    sib_s, sib_r = Slots(sib_s, SIB_SEMS), Slots(sib_r, SIB_SEMS)
    g_s, g_r = Slots(g_s, G_SEMS), Slots(g_r, G_SEMS)
    ps_s, ps_r = Slots(ps_s, PS_SEMS), Slots(ps_r, PS_SEMS)
    rs_s, rs_r = Slots(rs_s, RS_SEMS), Slots(rs_r, RS_SEMS)
    local = Slots(local, LOCAL_SEMS)

    barrier = pltpu.get_barrier_semaphore()
    neighbours = [sibling] + [towards(axis, step) for axis in "xyz" for step in (1, -1)]
    for there in neighbours:
        pl.semaphore_signal(barrier, inc=1, device_id=there, device_id_type=MESH)

    own_row = pl.multiple_of((dep * 8 + row) * TOK, 16)
    loads = {
        "pre": pltpu.make_async_copy(pre_hbm, pre, local["pre"]),
        "gh": pltpu.make_async_copy(gh_hbm, gh, local["gh"]),
        "x0": pltpu.make_async_copy(x_hbm.at[:, pl.ds(0, HALF)], xall.at[0, pl.ds(own_row, TOK)], local["x0"]),
        "x1": pltpu.make_async_copy(x_hbm.at[:, pl.ds(HALF, HALF)], xall.at[1, pl.ds(own_row, TOK)], local["x1"]),
        "w": pltpu.make_async_copy(w_hbm, w, local["w"]),
    }
    for name in ("x0", "x1", "pre", "gh", "w"):
        loads[name].start()

    pending = []

    def send(src, dst, s, r, there):
        copy = pltpu.make_async_remote_copy(
            src_ref=src, dst_ref=dst, send_sem=s, recv_sem=r, device_id=there, device_id_type=MESH
        )
        copy.start()
        return copy

    def arrived(dst, s, r):
        pltpu.make_async_remote_copy(
            src_ref=dst, dst_ref=dst, send_sem=s, recv_sem=r, device_id=sibling, device_id_type=MESH
        ).wait_recv()

    def drain(left):
        while len(pending) > left:
            pending.pop(0).wait_send()

    axes = (("y", "z"), ("z", "y"))

    def x_rows(h, o1, o2, of_core):
        first, second = (place[axes[h][0]] + o1) % N, (place[axes[h][1]] + o2) % N
        yy, zz = (first, second) if h == 0 else (second, first)
        return pl.multiple_of((((zz % 2) * 2 + of_core) * 8 + yy * 2 + zz // 2) * TOK, 16)

    def x_block(h, o1, o2, sub, of_core):
        rows = pl.ds(x_rows(h, o1, o2, of_core), TOK)
        if sub is None:
            return xall.at[h, rows]
        return xall.at[h, rows, pl.ds(sub * SUB, SUB)]

    def x_send(h, o1, o2, sub, along, step):
        block = x_block(h, o1, o2, sub, core)
        there = ((o1 - step) % N, o2) if along == 0 else (o1, (o2 - step) % N)
        pending.append(
            send(block, block, ag_s[h, o1, o2, sub, along, step], ag_r[(h, *there, sub)], towards(axes[h][along], step))
        )

    def x_send_own(h, along, step):
        there = (-step % N, 0) if along == 0 else (0, -step % N)
        pending.append(send(
            x_hbm.at[:, pl.ds(h * HALF, HALF)], x_block(h, 0, 0, None, core),
            ag_s[h, 0, 0, None, along, step], ag_r[(h, *there, None)], towards(axes[h][along], step),
        ))

    def x_arrived(h, o1, o2, sub):
        arrived(x_block(h, o1, o2, sub, core), ag_s[h, 0, 0, None, 0, 1], ag_r[h, o1, o2, sub])

    def x_share(h, o1, o2):
        block = x_block(h, o1, o2, None, core)
        pending.append(send(block, block, sib_s[h, o1, o2], sib_r[h, o1, o2], sibling))

    def x_shared(h, o1, o2):
        arrived(x_block(h, o1, o2, None, 1 - core), sib_s[h, 0, 0], sib_r[h, o1, o2])

    def x_first(h, o1):
        x_arrived(h, o1, 0, None)
        x_send(h, o1, 0, 0 if o1 == 3 else 1, 0, 1 if o1 == 3 else -1)

    def x_turn(h, o1):
        for step in (1, -1):
            x_send(h, o1, 0, None, 1, step)
        x_share(h, o1, 0)

    def x_far(h):
        for sub in (0, 1):
            x_arrived(h, 2, 0, sub)
            x_send(h, 2, 0, sub, 1, 1)
            x_send(h, 2, 0, sub, 1, -1)
        x_share(h, 2, 0)

    def x_second(h, o1):
        if o1 == 2:
            for o2, sub in ((3, 0), (1, 1)):
                x_arrived(h, 2, o2, sub)
                x_send(h, 2, o2, sub, 1, 1 if o2 == 3 else -1)
            for o2, sub in ((3, 1), (1, 0)):
                x_arrived(h, 2, o2, sub)
                x_share(h, 2, o2)
            return
        for o2 in (3, 1):
            x_arrived(h, o1, o2, None)
            x_send(h, o1, o2, 0 if o2 == 3 else 1, 1, 1 if o2 == 3 else -1)
            x_share(h, o1, o2)

    def x_last(h, o1):
        for sub in (0, 1):
            x_arrived(h, o1, 2, sub)
        x_share(h, o1, 2)

    def g_block(o, q):
        return gall.at[pl.ds(pl.multiple_of(((x + o) % N) * BLOCK + q * CHUNK, 16), CHUNK)]

    def g_send(o, q, step):
        block = g_block(o, q)
        pending.append(send(block, block, g_s[o, q, step], g_r[(o - step) % N, q], towards("x", step)))

    def g_arrived(o, q):
        arrived(g_block(o, q), g_s[0, 0, 1], g_r[o, q])

    def g_forward(o, q):
        g_arrived(o, q)
        g_send(o, q, 1 if o == 3 else -1)

    def g_compute(q):
        @pl.loop(0, CHUNK // 32)
        def _(i):
            rows = pl.ds(pl.multiple_of(q * CHUNK + i * 32, 32), 32)
            slope = gelu_slope(pre[rows].astype(F32))
            value = (gh[rows].astype(F32) * slope).astype(BF)
            gall[pl.ds(pl.multiple_of(x * BLOCK + q * CHUNK + i * 32, 32), 32)] = value

    def partial(o, h):
        block = (x + o) % N
        away, z_of = (block + core) % 2, block // 2
        rows = pl.ds(pl.multiple_of(block * BLOCK, 16), BLOCK)
        @pl.loop(0, 2)
        def _(n):
            product = lax.dot_general(
                gall[rows],
                w[pl.ds(pl.multiple_of(h * HALF + n * SUB, SUB), SUB)],
                (((1,), (1,)), ((), ())),
                preferred_element_type=F32,
            )
            part[away, z_of, h, :, pl.ds(pl.multiple_of(n * SUB, SUB), SUB)] = product.astype(BF)

        @pl.when(away == 1)
        def _():
            for yy in range(N):
                piece = pl.ds(yy * CHUNK, CHUNK)
                slot = (o // 2 * 2 + h) * N + yy
                send(
                    part.at[1, z_of, h, piece], psib.at[z_of, h, piece],
                    ps_s.ref.at[slot], ps_r.ref.at[(z_of * 2 + h) * N + yy], sibling,
                )

    def sib_part(zl, h, yy):
        piece = psib.at[zl, h, pl.ds(pl.multiple_of(yy * CHUNK, 16), CHUNK)]
        arrived(piece, ps_s.ref.at[0], ps_r.ref.at[(zl * 2 + h) * N + yy])

    rs_axes = (("z", "y"), ("y", "z"))

    def target(h, oa, ob):
        a, b = (place[rs_axes[h][0]] + oa) % N, (place[rs_axes[h][1]] + ob) % N
        zz, yy = (a, b) if h == 0 else (b, a)
        return zz % 2, pl.multiple_of(yy * CHUNK + (zz // 2) * TOK, 16), yy

    def rows16(body):
        @pl.loop(0, TOK // 16)
        def _(i):
            body(pl.multiple_of(i * 16, 16))

    def whole(h, zl, row0, i):
        at = pl.ds(pl.multiple_of(row0 + i, 16), 16)
        return part[0, zl, h, at].astype(F32) + psib[zl, h, at].astype(F32)

    def first_step(h, ob):
        zl, row0, yy = target(h, 2, ob)
        if h == 0 or ob in (2, 1):
            sib_part(zl, h, yy)

        def add(i):
            part[0, zl, h, pl.ds(pl.multiple_of(row0 + i, 16), 16)] = whole(h, zl, row0, i).astype(BF)

        rows16(add)
        for sub, step in ((0, 1), (1, -1)):
            send(
                part.at[0, zl, h, pl.ds(row0, TOK), pl.ds(sub * SUB, SUB)], r1.at[h, sub, ob],
                rs_s[1, h, sub, ob], rs_r[1, h, sub, ob], towards(rs_axes[h][0], step),
            )

    def first_sent(h, ob):
        zl, row0, _ = target(h, 2, ob)
        for sub, step in ((0, 1), (1, -1)):
            pending.append(pltpu.make_async_remote_copy(
                src_ref=part.at[0, zl, h, pl.ds(row0, TOK), pl.ds(sub * SUB, SUB)], dst_ref=r1.at[h, sub, ob],
                send_sem=rs_s[1, h, sub, ob], recv_sem=rs_r[1, h, sub, ob],
                device_id=towards(rs_axes[h][0], step), device_id_type=MESH,
            ))

    def second_step(h, ob):
        for sub, oa, step in ((0, 1, 1), (1, 3, -1)):
            zl, row0, yy = target(h, oa, ob)
            if (h == 0 and sub == 0) or (h == 1 and ob in (2, 1)):
                sib_part(zl, h, yy)
            arrived(r1.at[h, sub, ob], rs_s[1, h, sub, ob], rs_r[1, h, sub, ob])
            got, kept = pl.ds(sub * SUB, SUB), pl.ds((1 - sub) * SUB, SUB)

            def add(i):
                at = pl.ds(pl.multiple_of(row0 + i, 16), 16)
                part[0, zl, h, at, got] = (
                    part[0, zl, h, at, got].astype(F32) + psib[zl, h, at, got].astype(F32)
                    + r1[h, sub, ob, pl.ds(i, 16)].astype(F32)
                ).astype(BF)
                part[0, zl, h, at, kept] = (
                    part[0, zl, h, at, kept].astype(F32) + psib[zl, h, at, kept].astype(F32)
                ).astype(BF)

            rows16(add)
            pending.append(send(
                part.at[0, zl, h, pl.ds(row0, TOK)], r2.at[h, sub, ob],
                rs_s[2, h, sub, ob], rs_r[2, h, sub, ob], towards(rs_axes[h][0], step),
            ))

    def third_step(h, ob):
        zl, row0, yy = target(h, 0, ob)
        if h == 1 and ob in (2, 1):
            sib_part(zl, h, yy)
        for sub in (0, 1):
            arrived(r2.at[h, sub, ob], rs_s[2, h, sub, ob], rs_r[2, h, sub, ob])

        def add(i):
            at, here = pl.ds(i, 16), pl.ds(pl.multiple_of(row0 + i, 16), 16)
            total = whole(h, zl, row0, i) + r2[h, 0, ob, at].astype(F32) + r2[h, 1, ob, at].astype(F32)
            if ob == 0:
                own[h, at] = total
            elif ob == 2:
                part[0, zl, h, here] = total.astype(BF)
            else:
                sub = 0 if ob == 1 else 1
                onward[h, sub, at] = total[:, sub * SUB:(sub + 1) * SUB]
                part[0, zl, h, here, pl.ds((1 - sub) * SUB, SUB)] = (
                    total[:, (1 - sub) * SUB:(2 - sub) * SUB].astype(BF)
                )

        rows16(add)

    def fourth_step(h):
        zl, row0, _ = target(h, 0, 2)
        for sub, step in ((0, 1), (1, -1)):
            pending.append(send(
                part.at[0, zl, h, pl.ds(row0, TOK), pl.ds(sub * SUB, SUB)], r3.at[h, sub],
                rs_s[3, h, sub], rs_r[3, h, sub], towards(rs_axes[h][1], step),
            ))

    def fifth_step_early(h, sub):
        ob, step = ((1, 1), (3, -1))[sub]
        zl, row0, _ = target(h, 0, ob)
        kept = pl.ds((1 - sub) * SUB, SUB)
        pending.append(send(
            part.at[0, zl, h, pl.ds(row0, TOK), kept], r4.at[h, sub, :, kept],
            rs_s[4, h, sub, 1], rs_r[4, h, sub, 1], towards(rs_axes[h][1], step),
        ))

    def fifth_step(h, sub):
        ob, step = ((1, 1), (3, -1))[sub]
        zl, row0, _ = target(h, 0, ob)
        got = pl.ds(sub * SUB, SUB)
        arrived(r3.at[h, sub], rs_s[3, h, sub], rs_r[3, h, sub])

        def add(i):
            at = pl.ds(i, 16)
            part[0, zl, h, pl.ds(pl.multiple_of(row0 + i, 16), 16), got] = (
                onward[h, sub, at] + r3[h, sub, at].astype(F32)
            ).astype(BF)

        rows16(add)
        pending.append(send(
            part.at[0, zl, h, pl.ds(row0, TOK), got], r4.at[h, sub, :, got],
            rs_s[4, h, sub, 0], rs_r[4, h, sub, 0], towards(rs_axes[h][1], step),
        ))

    def sixth_step_early(h):
        for sub in (0, 1):
            kept = pl.ds((1 - sub) * SUB, SUB)
            arrived(r4.at[h, sub, :, kept], rs_s[4, h, sub, 1], rs_r[4, h, sub, 1])

            def add(i):
                at = pl.ds(i, 16)
                own[h, at, kept] = own[h, at, kept] + r4[h, sub, at, kept].astype(F32)

            rows16(add)

    def sixth_step(h, sub):
        got = pl.ds(sub * SUB, SUB)
        arrived(r4.at[h, sub, :, got], rs_s[4, h, sub, 0], rs_r[4, h, sub, 0])

        def add(i):
            at = pl.ds(i, 16)
            gi_ref[at, pl.ds(h * HALF + sub * SUB, SUB)] = (
                own[h, at, got] + r4[h, sub, at, got].astype(F32)
            ).astype(BF)

        rows16(add)

    tiles = HALF // GTILE

    def weight_tile(n):
        h, m = n // tiles, n % tiles
        product = lax.dot_general(
            xall[h, :, pl.ds(m * GTILE, GTILE)], gall[...], (((0,), (0,)), ((), ())), preferred_element_type=F32
        )
        rows = pl.ds(n * GTILE, GTILE)
        gwb[rows] = product.astype(BF)

    both = (0, 1)
    pl.semaphore_wait(barrier, len(neighbours))
    for along in (0, 1):
        for h in both:
            for step in (1, -1):
                x_send_own(h, along, step)
    loads["pre"].wait()
    loads["gh"].wait()
    for q in (0, 2, 1, 3):
        g_compute(q)
        g_send(0, q, 1)
        g_send(0, q, -1)
    loads["x0"].wait()
    loads["x1"].wait()
    for h in both:
        x_share(h, 0, 0)
    loads["w"].wait()
    for h in both:
        partial(0, h)
    for o in (3, 1):
        for h in both:
            x_first(h, o)
    for o in (3, 1):
        for h in both:
            x_turn(h, o)
    g_forward(3, 0)
    g_forward(1, 2)
    for h in both:
        x_second(h, 0)
    g_forward(3, 1)
    g_forward(1, 3)
    for h in both:
        x_far(h)
    for h in both:
        x_second(h, 3)
    for q in (2, 3):
        g_arrived(3, q)
    partial(3, 0)
    for h in both:
        x_second(h, 1)
    partial(3, 1)
    for q in (0, 1):
        g_arrived(1, q)
    partial(1, 0)
    for h in both:
        x_last(h, 0)
    partial(1, 1)
    odd = x % 2 == 1
    lead = jnp.logical_and(core == 0, odd)
    lead_own = jnp.logical_and(core == 0, x % 2 == 0)

    def owned(h, ob):
        return (z + (ob if h == 1 else 2)) % 2 == x // 2

    def first_steps(halves, when):
        for h in halves:
            for ob in (2, 1, 3, 0):
                pl.when(when(h, ob))(functools.partial(first_step, h, ob))

    def first_sends():
        for h in both:
            for ob in (2, 1, 3, 0):
                first_sent(h, ob)

    for h in both:
        x_second(h, 2)
    first_steps(both, lambda h, ob: jnp.logical_and(lead_own, owned(h, ob)))
    pl.when(lead)(lambda: first_steps((0,), lambda h, ob: True))
    for q in range(4):
        g_arrived(2, q)
    partial(2, 0)
    pl.when(lead)(lambda: first_steps((1,), lambda h, ob: True))
    partial(2, 1)
    first_steps(
        both, lambda h, ob: jnp.logical_or(core == 1, jnp.logical_and(lead_own, jnp.logical_not(owned(h, ob))))
    )
    first_sends()
    for ob in (2, 1, 3):
        for h in both:
            second_step(h, ob)
    for o1 in (3, 1, 2):
        for h in both:
            x_last(h, o1)
    for o1 in range(N):
        for o2 in range(N):
            for h in both:
                x_shared(h, o1, o2)
    weight_tile(0)
    weight_tile(1)
    for h in both:
        third_step(h, 2)
        fourth_step(h)
    for h in both:
        second_step(h, 0)
    weight_tile(2)
    weight_tile(3)
    for h in both:
        third_step(h, 1)
        fifth_step_early(h, 0)
    weight_tile(4)
    for h in both:
        third_step(h, 3)
        fifth_step_early(h, 1)
    weight_tile(5)
    for slot in range(PS_SEMS):
        piece = part.at[1, 0, 0, pl.ds(0, CHUNK)]
        pltpu.make_async_remote_copy(
            src_ref=piece, dst_ref=piece, send_sem=ps_s.ref.at[slot], recv_sem=ps_r.ref.at[0],
            device_id=sibling, device_id_type=MESH,
        ).wait_send()
    for h in both:
        for sub in (0, 1):
            fifth_step(h, sub)
    drain(12)
    for h in both:
        third_step(h, 0)
    for h in both:
        sixth_step_early(h)
    for sub in (0, 1):
        for h in both:
            sixth_step(h, sub)
    drain(0)


def write_out(gi, gw, gi_hbm, gw_hbm, sems):
    rows = FEAT // WRITES
    copies = [pltpu.make_async_copy(gi, gi_hbm, sems.at[WRITES])]
    for n in range(WRITES):
        part = pl.ds(n * rows, rows)
        copies.append(pltpu.make_async_copy(gw.at[part], gw_hbm.at[part], sems.at[n]))
    for copy in copies:
        copy.start()
    for copy in copies:
        copy.wait()


def per_device(inputs, weight, pre_act, grad_hidden):
    dma = pltpu.SemaphoreType.DMA
    grads = pl.pallas_call(
        kernel,
        out_shape=(pltpu.VMEM((TOK, FEAT), BF), pltpu.VMEM((FEAT, HID), BF)),
        in_specs=[pl.BlockSpec(memory_space=pl.ANY)] * 4,
        out_specs=(pl.BlockSpec(memory_space=pltpu.VMEM), pl.BlockSpec(memory_space=pltpu.VMEM)),
        scratch_shapes=[
            pltpu.VMEM((2, N * BLOCK, HALF), BF),
            pltpu.VMEM((N * BLOCK, HID), BF),
            pltpu.VMEM((BLOCK, HID), BF),
            pltpu.VMEM((BLOCK, HID), BF),
            pltpu.VMEM((FEAT, HID), BF),
            pltpu.VMEM((2, 2, 2, BLOCK, HALF), BF),
            pltpu.VMEM((2, 2, BLOCK, HALF), BF),
            pltpu.VMEM((2, 2, N, TOK, SUB), BF),
            pltpu.VMEM((2, 2, N, TOK, HALF), BF),
            pltpu.VMEM((2, 2, TOK, SUB), BF),
            pltpu.VMEM((2, 2, TOK, HALF), BF),
            pltpu.VMEM((2, TOK, HALF), F32),
            pltpu.VMEM((2, 2, TOK, SUB), F32),
            dma((64,)), dma((AG_SEMS,)),
            dma((SIB_SEMS,)), dma((SIB_SEMS,)),
            dma((G_SEMS,)), dma((G_SEMS,)),
            dma((PS_SEMS,)), dma((PS_SEMS,)),
            dma((RS_SEMS,)), dma((RS_SEMS,)),
            dma((LOCAL_SEMS,)),
        ],
        compiler_params=pltpu.CompilerParams(
            collective_id=0, has_side_effects=True, vmem_limit_bytes=50 << 20
        ),
        cost_estimate=pl.CostEstimate(flops=14_500_000_000, bytes_accessed=16_000_000, transcendentals=300_000),
        name="gelu_up_backward",
    )(inputs, weight, pre_act, grad_hidden)
    return pl.pallas_call(
        write_out,
        out_shape=tuple(jax.ShapeDtypeStruct(g.shape, g.dtype) for g in grads),
        in_specs=[pl.BlockSpec(memory_space=pltpu.VMEM)] * 2,
        out_specs=[pl.BlockSpec(memory_space=pl.ANY)] * 2,
        scratch_shapes=[dma((1 + WRITES,))],
        compiler_params=pltpu.CompilerParams(vmem_limit_bytes=1 << 20),
        name="write_out",
    )(*(pltpu.with_memory_space_constraint(g, pltpu.VMEM) for g in grads))


def solution(mesh):
    return jax.shard_map(
        per_device,
        mesh=mesh,
        in_specs=(
            P(("depth", "row"), "col"),
            P("col", ("depth", "row")),
            P("col", ("depth", "row")),
            P("col", ("depth", "row")),
        ),
        out_specs=(P(("depth", "row"), "col"), P("col", ("depth", "row"))),
        check_vma=False,
    )
```

```python
import functools
import math

import jax
import jax.numpy as jnp
from jax import lax
from jax.experimental import pallas as pl
from jax.experimental.pallas import tpu as pltpu
from jax.sharding import PartitionSpec as P

MESH = pl.DeviceIdType.MESH
BF, F32 = jnp.bfloat16, jnp.float32

N = 4
TOK = 48
HALF = 1536
SUB = HALF // 2
FEAT = 2 * HALF
HID = 768
BLOCK = 384
CHUNK = 96
GTILE = 512
WRITES = 4


def gelu_slope(pre):
    coeff = math.sqrt(2.0 / math.pi)
    inner = coeff * (pre + 0.044715 * pre * pre * pre)
    tanh_val = jnp.tanh(inner)
    return 0.5 * (1.0 + tanh_val) + 0.5 * pre * (1.0 - tanh_val * tanh_val) * coeff * (
        1.0 + 3.0 * 0.044715 * pre * pre
    )


class Slots:
    def __init__(self, ref, size):
        self.ref, self.size, self.keys = ref, size, {}

    def __getitem__(self, key):
        place = self.keys.setdefault(key, len(self.keys))
        assert place < self.size
        return self.ref.at[place]


AG_SEMS, SIB_SEMS, G_SEMS, PS_SEMS, RS_SEMS, LOCAL_SEMS = 44, 32, 12, 16, 44, 16


def kernel(
    x_hbm, w_hbm, pre_hbm, gh_hbm, gi_ref, gwb,
    xall, gall, pre, gh, w, part, psib, r1, r2, r3, r4, own, onward,
    ag_s, ag_r, sib_s, sib_r, g_s, g_r, ps_s, ps_r, rs_s, rs_r, local,
):
    dep, row, x = lax.axis_index("depth"), lax.axis_index("row"), lax.axis_index("col")
    z_lo, core = dep // 2, dep % 2
    y, z = row // 2, (row % 2) * 2 + z_lo
    place = {"x": x, "y": y, "z": z}

    def device(x, y, z, core):
        return ((z % 2) * 2 + core, y * 2 + z // 2, x)

    def towards(axis, step):
        there = dict(place)
        there[axis] = (place[axis] + step) % N
        return device(there["x"], there["y"], there["z"], core)

    sibling = device(x, y, z, 1 - core)

    ag_s, ag_r = Slots(ag_s, 64), Slots(ag_r, AG_SEMS)
    sib_s, sib_r = Slots(sib_s, SIB_SEMS), Slots(sib_r, SIB_SEMS)
    g_s, g_r = Slots(g_s, G_SEMS), Slots(g_r, G_SEMS)
    ps_s, ps_r = Slots(ps_s, PS_SEMS), Slots(ps_r, PS_SEMS)
    rs_s, rs_r = Slots(rs_s, RS_SEMS), Slots(rs_r, RS_SEMS)
    local = Slots(local, LOCAL_SEMS)

    barrier = pltpu.get_barrier_semaphore()
    neighbours = [sibling] + [towards(axis, step) for axis in "xyz" for step in (1, -1)]
    for there in neighbours:
        pl.semaphore_signal(barrier, inc=1, device_id=there, device_id_type=MESH)

    own_row = pl.multiple_of((dep * 8 + row) * TOK, 16)
    loads = {
        "pre": pltpu.make_async_copy(pre_hbm, pre, local["pre"]),
        "gh": pltpu.make_async_copy(gh_hbm, gh, local["gh"]),
        "x0": pltpu.make_async_copy(x_hbm.at[:, pl.ds(0, HALF)], xall.at[0, pl.ds(own_row, TOK)], local["x0"]),
        "x1": pltpu.make_async_copy(x_hbm.at[:, pl.ds(HALF, HALF)], xall.at[1, pl.ds(own_row, TOK)], local["x1"]),
        "w": pltpu.make_async_copy(w_hbm, w, local["w"]),
    }
    for name in ("x0", "x1", "pre", "gh", "w"):
        loads[name].start()

    pending = []

    def send(src, dst, s, r, there):
        copy = pltpu.make_async_remote_copy(
            src_ref=src, dst_ref=dst, send_sem=s, recv_sem=r, device_id=there, device_id_type=MESH
        )
        copy.start()
        return copy

    def arrived(dst, s, r):
        pltpu.make_async_remote_copy(
            src_ref=dst, dst_ref=dst, send_sem=s, recv_sem=r, device_id=sibling, device_id_type=MESH
        ).wait_recv()

    def drain(left):
        while len(pending) > left:
            pending.pop(0).wait_send()

    axes = (("y", "z"), ("z", "y"))

    def x_rows(h, o1, o2, of_core):
        first, second = (place[axes[h][0]] + o1) % N, (place[axes[h][1]] + o2) % N
        yy, zz = (first, second) if h == 0 else (second, first)
        return pl.multiple_of((((zz % 2) * 2 + of_core) * 8 + yy * 2 + zz // 2) * TOK, 16)

    def x_block(h, o1, o2, sub, of_core):
        rows = pl.ds(x_rows(h, o1, o2, of_core), TOK)
        if sub is None:
            return xall.at[h, rows]
        return xall.at[h, rows, pl.ds(sub * SUB, SUB)]

    def x_send(h, o1, o2, sub, along, step):
        block = x_block(h, o1, o2, sub, core)
        there = ((o1 - step) % N, o2) if along == 0 else (o1, (o2 - step) % N)
        pending.append(
            send(block, block, ag_s[h, o1, o2, sub, along, step], ag_r[(h, *there, sub)], towards(axes[h][along], step))
        )

    def x_send_own(h, along, step):
        there = (-step % N, 0) if along == 0 else (0, -step % N)
        pending.append(send(
            x_hbm.at[:, pl.ds(h * HALF, HALF)], x_block(h, 0, 0, None, core),
            ag_s[h, 0, 0, None, along, step], ag_r[(h, *there, None)], towards(axes[h][along], step),
        ))

    def x_arrived(h, o1, o2, sub):
        arrived(x_block(h, o1, o2, sub, core), ag_s[h, 0, 0, None, 0, 1], ag_r[h, o1, o2, sub])

    def x_share(h, o1, o2):
        block = x_block(h, o1, o2, None, core)
        pending.append(send(block, block, sib_s[h, o1, o2], sib_r[h, o1, o2], sibling))

    def x_shared(h, o1, o2):
        arrived(x_block(h, o1, o2, None, 1 - core), sib_s[h, 0, 0], sib_r[h, o1, o2])

    def x_first(h, o1):
        x_arrived(h, o1, 0, None)
        x_send(h, o1, 0, 0 if o1 == 3 else 1, 0, 1 if o1 == 3 else -1)

    def x_turn(h, o1):
        for step in (1, -1):
            x_send(h, o1, 0, None, 1, step)
        x_share(h, o1, 0)

    def x_far(h):
        for sub in (0, 1):
            x_arrived(h, 2, 0, sub)
            x_send(h, 2, 0, sub, 1, 1)
            x_send(h, 2, 0, sub, 1, -1)
        x_share(h, 2, 0)

    def x_second(h, o1):
        if o1 == 2:
            for o2, sub in ((3, 0), (1, 1)):
                x_arrived(h, 2, o2, sub)
                x_send(h, 2, o2, sub, 1, 1 if o2 == 3 else -1)
            for o2, sub in ((3, 1), (1, 0)):
                x_arrived(h, 2, o2, sub)
                x_share(h, 2, o2)
            return
        for o2 in (3, 1):
            x_arrived(h, o1, o2, None)
            x_send(h, o1, o2, 0 if o2 == 3 else 1, 1, 1 if o2 == 3 else -1)
            x_share(h, o1, o2)

    def x_last(h, o1):
        for sub in (0, 1):
            x_arrived(h, o1, 2, sub)
        x_share(h, o1, 2)

    def g_block(o, q):
        return gall.at[pl.ds(pl.multiple_of(((x + o) % N) * BLOCK + q * CHUNK, 16), CHUNK)]

    def g_send(o, q, step):
        block = g_block(o, q)
        pending.append(send(block, block, g_s[o, q, step], g_r[(o - step) % N, q], towards("x", step)))

    def g_arrived(o, q):
        arrived(g_block(o, q), g_s[0, 0, 1], g_r[o, q])

    def g_forward(o, q):
        g_arrived(o, q)
        g_send(o, q, 1 if o == 3 else -1)

    def g_compute(q):
        @pl.loop(0, CHUNK // 32)
        def _(i):
            rows = pl.ds(pl.multiple_of(q * CHUNK + i * 32, 32), 32)
            slope = gelu_slope(pre[rows].astype(F32))
            value = (gh[rows].astype(F32) * slope).astype(BF)
            gall[pl.ds(pl.multiple_of(x * BLOCK + q * CHUNK + i * 32, 32), 32)] = value

    def partial(o, h):
        block = (x + o) % N
        away, z_of = (block + core) % 2, block // 2
        rows = pl.ds(pl.multiple_of(block * BLOCK, 16), BLOCK)
        @pl.loop(0, 2)
        def _(n):
            product = lax.dot_general(
                gall[rows],
                w[pl.ds(pl.multiple_of(h * HALF + n * SUB, SUB), SUB)],
                (((1,), (1,)), ((), ())),
                preferred_element_type=F32,
            )
            part[away, z_of, h, :, pl.ds(pl.multiple_of(n * SUB, SUB), SUB)] = product.astype(BF)

        @pl.when(away == 1)
        def _():
            for yy in range(N):
                piece = pl.ds(yy * CHUNK, CHUNK)
                slot = (o // 2 * 2 + h) * N + yy
                send(
                    part.at[1, z_of, h, piece], psib.at[z_of, h, piece],
                    ps_s.ref.at[slot], ps_r.ref.at[(z_of * 2 + h) * N + yy], sibling,
                )

    def sib_part(zl, h, yy):
        piece = psib.at[zl, h, pl.ds(pl.multiple_of(yy * CHUNK, 16), CHUNK)]
        arrived(piece, ps_s.ref.at[0], ps_r.ref.at[(zl * 2 + h) * N + yy])

    rs_axes = (("z", "y"), ("y", "z"))

    def target(h, oa, ob):
        a, b = (place[rs_axes[h][0]] + oa) % N, (place[rs_axes[h][1]] + ob) % N
        zz, yy = (a, b) if h == 0 else (b, a)
        return zz % 2, pl.multiple_of(yy * CHUNK + (zz // 2) * TOK, 16), yy

    def rows16(body):
        @pl.loop(0, TOK // 16)
        def _(i):
            body(pl.multiple_of(i * 16, 16))

    def whole(h, zl, row0, i):
        at = pl.ds(pl.multiple_of(row0 + i, 16), 16)
        return part[0, zl, h, at].astype(F32) + psib[zl, h, at].astype(F32)

    def first_step(h, ob):
        zl, row0, yy = target(h, 2, ob)
        if h == 0 or ob in (2, 1):
            sib_part(zl, h, yy)

        def add(i):
            part[0, zl, h, pl.ds(pl.multiple_of(row0 + i, 16), 16)] = whole(h, zl, row0, i).astype(BF)

        rows16(add)
        for sub, step in ((0, 1), (1, -1)):
            send(
                part.at[0, zl, h, pl.ds(row0, TOK), pl.ds(sub * SUB, SUB)], r1.at[h, sub, ob],
                rs_s[1, h, sub, ob], rs_r[1, h, sub, ob], towards(rs_axes[h][0], step),
            )

    def first_sent(h, ob):
        zl, row0, _ = target(h, 2, ob)
        for sub, step in ((0, 1), (1, -1)):
            pending.append(pltpu.make_async_remote_copy(
                src_ref=part.at[0, zl, h, pl.ds(row0, TOK), pl.ds(sub * SUB, SUB)], dst_ref=r1.at[h, sub, ob],
                send_sem=rs_s[1, h, sub, ob], recv_sem=rs_r[1, h, sub, ob],
                device_id=towards(rs_axes[h][0], step), device_id_type=MESH,
            ))

    def second_step(h, ob):
        for sub, oa, step in ((0, 1, 1), (1, 3, -1)):
            zl, row0, yy = target(h, oa, ob)
            if (h == 0 and sub == 0) or (h == 1 and ob in (2, 1)):
                sib_part(zl, h, yy)
            arrived(r1.at[h, sub, ob], rs_s[1, h, sub, ob], rs_r[1, h, sub, ob])
            got, kept = pl.ds(sub * SUB, SUB), pl.ds((1 - sub) * SUB, SUB)

            def add(i):
                at = pl.ds(pl.multiple_of(row0 + i, 16), 16)
                part[0, zl, h, at, got] = (
                    part[0, zl, h, at, got].astype(F32) + psib[zl, h, at, got].astype(F32)
                    + r1[h, sub, ob, pl.ds(i, 16)].astype(F32)
                ).astype(BF)
                part[0, zl, h, at, kept] = (
                    part[0, zl, h, at, kept].astype(F32) + psib[zl, h, at, kept].astype(F32)
                ).astype(BF)

            rows16(add)
            pending.append(send(
                part.at[0, zl, h, pl.ds(row0, TOK)], r2.at[h, sub, ob],
                rs_s[2, h, sub, ob], rs_r[2, h, sub, ob], towards(rs_axes[h][0], step),
            ))

    def third_step(h, ob):
        zl, row0, yy = target(h, 0, ob)
        if h == 1 and ob in (2, 1):
            sib_part(zl, h, yy)
        for sub in (0, 1):
            arrived(r2.at[h, sub, ob], rs_s[2, h, sub, ob], rs_r[2, h, sub, ob])

        def add(i):
            at, here = pl.ds(i, 16), pl.ds(pl.multiple_of(row0 + i, 16), 16)
            total = whole(h, zl, row0, i) + r2[h, 0, ob, at].astype(F32) + r2[h, 1, ob, at].astype(F32)
            if ob == 0:
                own[h, at] = total
            elif ob == 2:
                part[0, zl, h, here] = total.astype(BF)
            else:
                sub = 0 if ob == 1 else 1
                onward[h, sub, at] = total[:, sub * SUB:(sub + 1) * SUB]
                part[0, zl, h, here, pl.ds((1 - sub) * SUB, SUB)] = (
                    total[:, (1 - sub) * SUB:(2 - sub) * SUB].astype(BF)
                )

        rows16(add)

    def fourth_step(h):
        zl, row0, _ = target(h, 0, 2)
        for sub, step in ((0, 1), (1, -1)):
            pending.append(send(
                part.at[0, zl, h, pl.ds(row0, TOK), pl.ds(sub * SUB, SUB)], r3.at[h, sub],
                rs_s[3, h, sub], rs_r[3, h, sub], towards(rs_axes[h][1], step),
            ))

    def fifth_step_early(h, sub):
        ob, step = ((1, 1), (3, -1))[sub]
        zl, row0, _ = target(h, 0, ob)
        kept = pl.ds((1 - sub) * SUB, SUB)
        pending.append(send(
            part.at[0, zl, h, pl.ds(row0, TOK), kept], r4.at[h, sub, :, kept],
            rs_s[4, h, sub, 1], rs_r[4, h, sub, 1], towards(rs_axes[h][1], step),
        ))

    def fifth_step(h, sub):
        ob, step = ((1, 1), (3, -1))[sub]
        zl, row0, _ = target(h, 0, ob)
        got = pl.ds(sub * SUB, SUB)
        arrived(r3.at[h, sub], rs_s[3, h, sub], rs_r[3, h, sub])

        def add(i):
            at = pl.ds(i, 16)
            part[0, zl, h, pl.ds(pl.multiple_of(row0 + i, 16), 16), got] = (
                onward[h, sub, at] + r3[h, sub, at].astype(F32)
            ).astype(BF)

        rows16(add)
        pending.append(send(
            part.at[0, zl, h, pl.ds(row0, TOK), got], r4.at[h, sub, :, got],
            rs_s[4, h, sub, 0], rs_r[4, h, sub, 0], towards(rs_axes[h][1], step),
        ))

    def sixth_step_early(h):
        for sub in (0, 1):
            kept = pl.ds((1 - sub) * SUB, SUB)
            arrived(r4.at[h, sub, :, kept], rs_s[4, h, sub, 1], rs_r[4, h, sub, 1])

            def add(i):
                at = pl.ds(i, 16)
                own[h, at, kept] = own[h, at, kept] + r4[h, sub, at, kept].astype(F32)

            rows16(add)

    def sixth_step(h, sub):
        got = pl.ds(sub * SUB, SUB)
        arrived(r4.at[h, sub, :, got], rs_s[4, h, sub, 0], rs_r[4, h, sub, 0])

        def add(i):
            at = pl.ds(i, 16)
            gi_ref[at, pl.ds(h * HALF + sub * SUB, SUB)] = (
                own[h, at, got] + r4[h, sub, at, got].astype(F32)
            ).astype(BF)

        rows16(add)

    tiles = HALF // GTILE

    def weight_tile(n):
        h, m = n // tiles, n % tiles
        product = lax.dot_general(
            xall[h, :, pl.ds(m * GTILE, GTILE)], gall[...], (((0,), (0,)), ((), ())), preferred_element_type=F32
        )
        rows = pl.ds(n * GTILE, GTILE)
        gwb[rows] = product.astype(BF)

    both = (0, 1)
    pl.semaphore_wait(barrier, len(neighbours))
    for along in (0, 1):
        for h in both:
            for step in (1, -1):
                x_send_own(h, along, step)
    loads["pre"].wait()
    loads["gh"].wait()
    for q in (0, 2, 1, 3):
        g_compute(q)
        g_send(0, q, 1)
        g_send(0, q, -1)
    loads["x0"].wait()
    loads["x1"].wait()
    for h in both:
        x_share(h, 0, 0)
    loads["w"].wait()
    for h in both:
        partial(0, h)
    for o in (3, 1):
        for h in both:
            x_first(h, o)
    for o in (3, 1):
        for h in both:
            x_turn(h, o)
    g_forward(3, 0)
    g_forward(1, 2)
    for h in both:
        x_second(h, 0)
    g_forward(3, 1)
    g_forward(1, 3)
    for h in both:
        x_far(h)
    for h in both:
        x_second(h, 3)
    for q in (2, 3):
        g_arrived(3, q)
    partial(3, 0)
    for h in both:
        x_second(h, 1)
    partial(3, 1)
    for q in (0, 1):
        g_arrived(1, q)
    partial(1, 0)
    for h in both:
        x_last(h, 0)
    partial(1, 1)
    odd = x % 2 == 1
    lead = jnp.logical_and(core == 0, odd)
    lead_own = (x + core) % 2 == 0
    last = jnp.logical_and(core == 1, x % 2 == 0)

    def owned(h, ob):
        return (z + (ob if h == 1 else 2)) % 2 == x // 2

    def first_steps(halves, when):
        for h in halves:
            for ob in (2, 1, 3, 0):
                pl.when(when(h, ob))(functools.partial(first_step, h, ob))

    def first_sends():
        for h in both:
            for ob in (2, 1, 3, 0):
                first_sent(h, ob)

    for h in both:
        x_second(h, 2)
    first_steps(both, lambda h, ob: jnp.logical_and(lead_own, owned(h, ob)))
    pl.when(lead)(lambda: first_steps((0,), lambda h, ob: True))
    for q in range(4):
        g_arrived(2, q)
    partial(2, 0)
    pl.when(lead)(lambda: first_steps((1,), lambda h, ob: True))
    partial(2, 1)
    first_steps(
        both, lambda h, ob: jnp.logical_or(last, jnp.logical_and(lead_own, jnp.logical_not(owned(h, ob))))
    )
    first_sends()
    for ob in (2, 1, 3):
        for h in both:
            second_step(h, ob)
    for o1 in (3, 1, 2):
        for h in both:
            x_last(h, o1)
    for o1 in range(N):
        for o2 in range(N):
            for h in both:
                x_shared(h, o1, o2)
    weight_tile(0)
    weight_tile(1)
    for h in both:
        third_step(h, 2)
        fourth_step(h)
    for h in both:
        second_step(h, 0)
    weight_tile(2)
    weight_tile(3)
    for h in both:
        third_step(h, 1)
        fifth_step_early(h, 0)
    weight_tile(4)
    for h in both:
        third_step(h, 3)
        fifth_step_early(h, 1)
    weight_tile(5)
    for slot in range(PS_SEMS):
        piece = part.at[1, 0, 0, pl.ds(0, CHUNK)]
        pltpu.make_async_remote_copy(
            src_ref=piece, dst_ref=piece, send_sem=ps_s.ref.at[slot], recv_sem=ps_r.ref.at[0],
            device_id=sibling, device_id_type=MESH,
        ).wait_send()
    for h in both:
        for sub in (0, 1):
            fifth_step(h, sub)
    drain(12)
    for h in both:
        third_step(h, 0)
    for h in both:
        sixth_step_early(h)
    for sub in (0, 1):
        for h in both:
            sixth_step(h, sub)
    drain(0)


def write_out(gi, gw, gi_hbm, gw_hbm, sems):
    rows = FEAT // WRITES
    copies = [pltpu.make_async_copy(gi, gi_hbm, sems.at[WRITES])]
    for n in range(WRITES):
        part = pl.ds(n * rows, rows)
        copies.append(pltpu.make_async_copy(gw.at[part], gw_hbm.at[part], sems.at[n]))
    for copy in copies:
        copy.start()
    for copy in copies:
        copy.wait()


def per_device(inputs, weight, pre_act, grad_hidden):
    dma = pltpu.SemaphoreType.DMA
    grads = pl.pallas_call(
        kernel,
        out_shape=(pltpu.VMEM((TOK, FEAT), BF), pltpu.VMEM((FEAT, HID), BF)),
        in_specs=[pl.BlockSpec(memory_space=pl.ANY)] * 4,
        out_specs=(pl.BlockSpec(memory_space=pltpu.VMEM), pl.BlockSpec(memory_space=pltpu.VMEM)),
        scratch_shapes=[
            pltpu.VMEM((2, N * BLOCK, HALF), BF),
            pltpu.VMEM((N * BLOCK, HID), BF),
            pltpu.VMEM((BLOCK, HID), BF),
            pltpu.VMEM((BLOCK, HID), BF),
            pltpu.VMEM((FEAT, HID), BF),
            pltpu.VMEM((2, 2, 2, BLOCK, HALF), BF),
            pltpu.VMEM((2, 2, BLOCK, HALF), BF),
            pltpu.VMEM((2, 2, N, TOK, SUB), BF),
            pltpu.VMEM((2, 2, N, TOK, HALF), BF),
            pltpu.VMEM((2, 2, TOK, SUB), BF),
            pltpu.VMEM((2, 2, TOK, HALF), BF),
            pltpu.VMEM((2, TOK, HALF), F32),
            pltpu.VMEM((2, 2, TOK, SUB), F32),
            dma((64,)), dma((AG_SEMS,)),
            dma((SIB_SEMS,)), dma((SIB_SEMS,)),
            dma((G_SEMS,)), dma((G_SEMS,)),
            dma((PS_SEMS,)), dma((PS_SEMS,)),
            dma((RS_SEMS,)), dma((RS_SEMS,)),
            dma((LOCAL_SEMS,)),
        ],
        compiler_params=pltpu.CompilerParams(
            collective_id=0, has_side_effects=True, vmem_limit_bytes=50 << 20
        ),
        cost_estimate=pl.CostEstimate(flops=14_500_000_000, bytes_accessed=16_000_000, transcendentals=300_000),
        name="gelu_up_backward",
    )(inputs, weight, pre_act, grad_hidden)
    return pl.pallas_call(
        write_out,
        out_shape=tuple(jax.ShapeDtypeStruct(g.shape, g.dtype) for g in grads),
        in_specs=[pl.BlockSpec(memory_space=pltpu.VMEM)] * 2,
        out_specs=[pl.BlockSpec(memory_space=pl.ANY)] * 2,
        scratch_shapes=[dma((1 + WRITES,))],
        compiler_params=pltpu.CompilerParams(vmem_limit_bytes=1 << 20),
        name="write_out",
    )(*(pltpu.with_memory_space_constraint(g, pltpu.VMEM) for g in grads))


def solution(mesh):
    return jax.shard_map(
        per_device,
        mesh=mesh,
        in_specs=(
            P(("depth", "row"), "col"),
            P("col", ("depth", "row")),
            P("col", ("depth", "row")),
            P("col", ("depth", "row")),
        ),
        out_specs=(P(("depth", "row"), "col"), P("col", ("depth", "row"))),
        check_vma=False,
    )
```

```python
import functools
import math

import jax
import jax.numpy as jnp
from jax import lax
from jax.experimental import pallas as pl
from jax.experimental.pallas import tpu as pltpu
from jax.sharding import PartitionSpec as P

MESH = pl.DeviceIdType.MESH
BF, F32 = jnp.bfloat16, jnp.float32

N = 4
TOK = 48
HALF = 1536
SUB = HALF // 2
FEAT = 2 * HALF
HID = 768
BLOCK = 384
CHUNK = 96
GTILE = 512
WRITES = 4


def gelu_slope(pre):
    coeff = math.sqrt(2.0 / math.pi)
    inner = coeff * (pre + 0.044715 * pre * pre * pre)
    tanh_val = jnp.tanh(inner)
    return 0.5 * (1.0 + tanh_val) + 0.5 * pre * (1.0 - tanh_val * tanh_val) * coeff * (
        1.0 + 3.0 * 0.044715 * pre * pre
    )


class Slots:
    def __init__(self, ref, size):
        self.ref, self.size, self.keys = ref, size, {}

    def __getitem__(self, key):
        place = self.keys.setdefault(key, len(self.keys))
        assert place < self.size
        return self.ref.at[place]


AG_SEMS, SIB_SEMS, G_SEMS, PS_SEMS, RS_SEMS, LOCAL_SEMS = 44, 32, 12, 16, 44, 16


def kernel(
    x_hbm, w_hbm, pre_hbm, gh_hbm, gi_ref, gwb,
    xall, gall, pre, gh, w, part, psib, r1, r2, r3, r4, own, onward,
    ag_s, ag_r, sib_s, sib_r, g_s, g_r, ps_s, ps_r, rs_s, rs_r, local,
):
    dep, row, x = lax.axis_index("depth"), lax.axis_index("row"), lax.axis_index("col")
    z_lo, core = dep // 2, dep % 2
    y, z = row // 2, (row % 2) * 2 + z_lo
    place = {"x": x, "y": y, "z": z}

    def device(x, y, z, core):
        return ((z % 2) * 2 + core, y * 2 + z // 2, x)

    def towards(axis, step):
        there = dict(place)
        there[axis] = (place[axis] + step) % N
        return device(there["x"], there["y"], there["z"], core)

    sibling = device(x, y, z, 1 - core)

    ag_s, ag_r = Slots(ag_s, 64), Slots(ag_r, AG_SEMS)
    sib_s, sib_r = Slots(sib_s, SIB_SEMS), Slots(sib_r, SIB_SEMS)
    g_s, g_r = Slots(g_s, G_SEMS), Slots(g_r, G_SEMS)
    ps_s, ps_r = Slots(ps_s, PS_SEMS), Slots(ps_r, PS_SEMS)
    rs_s, rs_r = Slots(rs_s, RS_SEMS), Slots(rs_r, RS_SEMS)
    local = Slots(local, LOCAL_SEMS)

    barrier = pltpu.get_barrier_semaphore()
    neighbours = [sibling] + [towards(axis, step) for axis in "xyz" for step in (1, -1)]
    for there in neighbours:
        pl.semaphore_signal(barrier, inc=1, device_id=there, device_id_type=MESH)

    own_row = pl.multiple_of((dep * 8 + row) * TOK, 16)
    loads = {
        "pre": pltpu.make_async_copy(pre_hbm, pre, local["pre"]),
        "gh": pltpu.make_async_copy(gh_hbm, gh, local["gh"]),
        "x0": pltpu.make_async_copy(x_hbm.at[:, pl.ds(0, HALF)], xall.at[0, pl.ds(own_row, TOK)], local["x0"]),
        "x1": pltpu.make_async_copy(x_hbm.at[:, pl.ds(HALF, HALF)], xall.at[1, pl.ds(own_row, TOK)], local["x1"]),
        "w": pltpu.make_async_copy(w_hbm, w, local["w"]),
    }
    for name in ("x0", "x1", "pre", "gh", "w"):
        loads[name].start()

    pending = []

    def send(src, dst, s, r, there):
        copy = pltpu.make_async_remote_copy(
            src_ref=src, dst_ref=dst, send_sem=s, recv_sem=r, device_id=there, device_id_type=MESH
        )
        copy.start()
        return copy

    def arrived(dst, s, r):
        pltpu.make_async_remote_copy(
            src_ref=dst, dst_ref=dst, send_sem=s, recv_sem=r, device_id=sibling, device_id_type=MESH
        ).wait_recv()

    def drain(left):
        while len(pending) > left:
            pending.pop(0).wait_send()

    axes = (("y", "z"), ("z", "y"))

    def x_rows(h, o1, o2, of_core):
        first, second = (place[axes[h][0]] + o1) % N, (place[axes[h][1]] + o2) % N
        yy, zz = (first, second) if h == 0 else (second, first)
        return pl.multiple_of((((zz % 2) * 2 + of_core) * 8 + yy * 2 + zz // 2) * TOK, 16)

    def x_block(h, o1, o2, sub, of_core):
        rows = pl.ds(x_rows(h, o1, o2, of_core), TOK)
        if sub is None:
            return xall.at[h, rows]
        return xall.at[h, rows, pl.ds(sub * SUB, SUB)]

    def x_send(h, o1, o2, sub, along, step):
        block = x_block(h, o1, o2, sub, core)
        there = ((o1 - step) % N, o2) if along == 0 else (o1, (o2 - step) % N)
        pending.append(
            send(block, block, ag_s[h, o1, o2, sub, along, step], ag_r[(h, *there, sub)], towards(axes[h][along], step))
        )

    def x_send_own(h, along, step):
        there = (-step % N, 0) if along == 0 else (0, -step % N)
        pending.append(send(
            x_hbm.at[:, pl.ds(h * HALF, HALF)], x_block(h, 0, 0, None, core),
            ag_s[h, 0, 0, None, along, step], ag_r[(h, *there, None)], towards(axes[h][along], step),
        ))

    def x_arrived(h, o1, o2, sub):
        arrived(x_block(h, o1, o2, sub, core), ag_s[h, 0, 0, None, 0, 1], ag_r[h, o1, o2, sub])

    def x_share(h, o1, o2):
        block = x_block(h, o1, o2, None, core)
        pending.append(send(block, block, sib_s[h, o1, o2], sib_r[h, o1, o2], sibling))

    def x_shared(h, o1, o2):
        arrived(x_block(h, o1, o2, None, 1 - core), sib_s[h, 0, 0], sib_r[h, o1, o2])

    def x_first(h, o1):
        x_arrived(h, o1, 0, None)
        x_send(h, o1, 0, 0 if o1 == 3 else 1, 0, 1 if o1 == 3 else -1)

    def x_turn(h, o1):
        for step in (1, -1):
            x_send(h, o1, 0, None, 1, step)
        x_share(h, o1, 0)

    def x_far(h):
        for sub in (0, 1):
            x_arrived(h, 2, 0, sub)
            x_send(h, 2, 0, sub, 1, 1)
            x_send(h, 2, 0, sub, 1, -1)
        x_share(h, 2, 0)

    def x_second(h, o1):
        if o1 == 2:
            for o2, sub in ((3, 0), (1, 1)):
                x_arrived(h, 2, o2, sub)
                x_send(h, 2, o2, sub, 1, 1 if o2 == 3 else -1)
            for o2, sub in ((3, 1), (1, 0)):
                x_arrived(h, 2, o2, sub)
                x_share(h, 2, o2)
            return
        for o2 in (3, 1):
            x_arrived(h, o1, o2, None)
            x_send(h, o1, o2, 0 if o2 == 3 else 1, 1, 1 if o2 == 3 else -1)
            x_share(h, o1, o2)

    def x_last(h, o1):
        for sub in (0, 1):
            x_arrived(h, o1, 2, sub)
        x_share(h, o1, 2)

    def g_block(o, q):
        return gall.at[pl.ds(pl.multiple_of(((x + o) % N) * BLOCK + q * CHUNK, 16), CHUNK)]

    def g_send(o, q, step):
        block = g_block(o, q)
        pending.append(send(block, block, g_s[o, q, step], g_r[(o - step) % N, q], towards("x", step)))

    def g_arrived(o, q):
        arrived(g_block(o, q), g_s[0, 0, 1], g_r[o, q])

    def g_forward(o, q):
        g_arrived(o, q)
        g_send(o, q, 1 if o == 3 else -1)

    def g_compute(q):
        @pl.loop(0, CHUNK // 32)
        def _(i):
            rows = pl.ds(pl.multiple_of(q * CHUNK + i * 32, 32), 32)
            slope = gelu_slope(pre[rows].astype(F32))
            value = (gh[rows].astype(F32) * slope).astype(BF)
            gall[pl.ds(pl.multiple_of(x * BLOCK + q * CHUNK + i * 32, 32), 32)] = value

    def partial(o, h):
        block = (x + o) % N
        away, z_of = (block + core) % 2, block // 2
        rows = pl.ds(pl.multiple_of(block * BLOCK, 16), BLOCK)
        @pl.loop(0, 2)
        def _(n):
            product = lax.dot_general(
                gall[rows],
                w[pl.ds(pl.multiple_of(h * HALF + n * SUB, SUB), SUB)],
                (((1,), (1,)), ((), ())),
                preferred_element_type=F32,
            )
            part[away, z_of, h, :, pl.ds(pl.multiple_of(n * SUB, SUB), SUB)] = product.astype(BF)

        @pl.when(away == 1)
        def _():
            for yy in range(N):
                piece = pl.ds(yy * CHUNK, CHUNK)
                slot = (o // 2 * 2 + h) * N + yy
                send(
                    part.at[1, z_of, h, piece], psib.at[z_of, h, piece],
                    ps_s.ref.at[slot], ps_r.ref.at[(z_of * 2 + h) * N + yy], sibling,
                )

    def sib_part(zl, h, yy):
        piece = psib.at[zl, h, pl.ds(pl.multiple_of(yy * CHUNK, 16), CHUNK)]
        arrived(piece, ps_s.ref.at[0], ps_r.ref.at[(zl * 2 + h) * N + yy])

    rs_axes = (("z", "y"), ("y", "z"))

    def target(h, oa, ob):
        a, b = (place[rs_axes[h][0]] + oa) % N, (place[rs_axes[h][1]] + ob) % N
        zz, yy = (a, b) if h == 0 else (b, a)
        return zz % 2, pl.multiple_of(yy * CHUNK + (zz // 2) * TOK, 16), yy

    def rows16(body):
        @pl.loop(0, TOK // 16)
        def _(i):
            body(pl.multiple_of(i * 16, 16))

    def whole(h, zl, row0, i):
        at = pl.ds(pl.multiple_of(row0 + i, 16), 16)
        return part[0, zl, h, at].astype(F32) + psib[zl, h, at].astype(F32)

    def first_step(h, ob):
        zl, row0, yy = target(h, 2, ob)
        if h == 0 or ob in (2, 1):
            sib_part(zl, h, yy)

        def add(i):
            part[0, zl, h, pl.ds(pl.multiple_of(row0 + i, 16), 16)] = whole(h, zl, row0, i).astype(BF)

        rows16(add)
        for sub, step in ((0, 1), (1, -1)):
            send(
                part.at[0, zl, h, pl.ds(row0, TOK), pl.ds(sub * SUB, SUB)], r1.at[h, sub, ob],
                rs_s[1, h, sub, ob], rs_r[1, h, sub, ob], towards(rs_axes[h][0], step),
            )

    def first_sent(h, ob):
        zl, row0, _ = target(h, 2, ob)
        for sub, step in ((0, 1), (1, -1)):
            pending.append(pltpu.make_async_remote_copy(
                src_ref=part.at[0, zl, h, pl.ds(row0, TOK), pl.ds(sub * SUB, SUB)], dst_ref=r1.at[h, sub, ob],
                send_sem=rs_s[1, h, sub, ob], recv_sem=rs_r[1, h, sub, ob],
                device_id=towards(rs_axes[h][0], step), device_id_type=MESH,
            ))

    def second_step(h, ob):
        for sub, oa, step in ((0, 1, 1), (1, 3, -1)):
            zl, row0, yy = target(h, oa, ob)
            if (h == 0 and sub == 0) or (h == 1 and ob in (2, 1)):
                sib_part(zl, h, yy)
            arrived(r1.at[h, sub, ob], rs_s[1, h, sub, ob], rs_r[1, h, sub, ob])
            got, kept = pl.ds(sub * SUB, SUB), pl.ds((1 - sub) * SUB, SUB)

            def add(i):
                at = pl.ds(pl.multiple_of(row0 + i, 16), 16)
                part[0, zl, h, at, got] = (
                    part[0, zl, h, at, got].astype(F32) + psib[zl, h, at, got].astype(F32)
                    + r1[h, sub, ob, pl.ds(i, 16)].astype(F32)
                ).astype(BF)
                part[0, zl, h, at, kept] = (
                    part[0, zl, h, at, kept].astype(F32) + psib[zl, h, at, kept].astype(F32)
                ).astype(BF)

            rows16(add)
            pending.append(send(
                part.at[0, zl, h, pl.ds(row0, TOK)], r2.at[h, sub, ob],
                rs_s[2, h, sub, ob], rs_r[2, h, sub, ob], towards(rs_axes[h][0], step),
            ))

    def third_step(h, ob):
        zl, row0, yy = target(h, 0, ob)
        if h == 1 and ob in (2, 1):
            sib_part(zl, h, yy)
        for sub in (0, 1):
            arrived(r2.at[h, sub, ob], rs_s[2, h, sub, ob], rs_r[2, h, sub, ob])

        def add(i):
            at, here = pl.ds(i, 16), pl.ds(pl.multiple_of(row0 + i, 16), 16)
            total = whole(h, zl, row0, i) + r2[h, 0, ob, at].astype(F32) + r2[h, 1, ob, at].astype(F32)
            if ob == 0:
                own[h, at] = total
            elif ob == 2:
                part[0, zl, h, here] = total.astype(BF)
            else:
                sub = 0 if ob == 1 else 1
                onward[h, sub, at] = total[:, sub * SUB:(sub + 1) * SUB]
                part[0, zl, h, here, pl.ds((1 - sub) * SUB, SUB)] = (
                    total[:, (1 - sub) * SUB:(2 - sub) * SUB].astype(BF)
                )

        rows16(add)

    def fourth_step(h):
        zl, row0, _ = target(h, 0, 2)
        for sub, step in ((0, 1), (1, -1)):
            pending.append(send(
                part.at[0, zl, h, pl.ds(row0, TOK), pl.ds(sub * SUB, SUB)], r3.at[h, sub],
                rs_s[3, h, sub], rs_r[3, h, sub], towards(rs_axes[h][1], step),
            ))

    def fifth_step_early(h, sub):
        ob, step = ((1, 1), (3, -1))[sub]
        zl, row0, _ = target(h, 0, ob)
        kept = pl.ds((1 - sub) * SUB, SUB)
        pending.append(send(
            part.at[0, zl, h, pl.ds(row0, TOK), kept], r4.at[h, sub, :, kept],
            rs_s[4, h, sub, 1], rs_r[4, h, sub, 1], towards(rs_axes[h][1], step),
        ))

    def fifth_step(h, sub):
        ob, step = ((1, 1), (3, -1))[sub]
        zl, row0, _ = target(h, 0, ob)
        got = pl.ds(sub * SUB, SUB)
        arrived(r3.at[h, sub], rs_s[3, h, sub], rs_r[3, h, sub])

        def add(i):
            at = pl.ds(i, 16)
            part[0, zl, h, pl.ds(pl.multiple_of(row0 + i, 16), 16), got] = (
                onward[h, sub, at] + r3[h, sub, at].astype(F32)
            ).astype(BF)

        rows16(add)
        pending.append(send(
            part.at[0, zl, h, pl.ds(row0, TOK), got], r4.at[h, sub, :, got],
            rs_s[4, h, sub, 0], rs_r[4, h, sub, 0], towards(rs_axes[h][1], step),
        ))

    def sixth_step_early(h):
        for sub in (0, 1):
            kept = pl.ds((1 - sub) * SUB, SUB)
            arrived(r4.at[h, sub, :, kept], rs_s[4, h, sub, 1], rs_r[4, h, sub, 1])

            def add(i):
                at = pl.ds(i, 16)
                own[h, at, kept] = own[h, at, kept] + r4[h, sub, at, kept].astype(F32)

            rows16(add)

    def sixth_step(h, sub):
        got = pl.ds(sub * SUB, SUB)
        arrived(r4.at[h, sub, :, got], rs_s[4, h, sub, 0], rs_r[4, h, sub, 0])

        def add(i):
            at = pl.ds(i, 16)
            gi_ref[at, pl.ds(h * HALF + sub * SUB, SUB)] = (
                own[h, at, got] + r4[h, sub, at, got].astype(F32)
            ).astype(BF)

        rows16(add)

    tiles = HALF // GTILE

    def weight_tile(n):
        h, m = n // tiles, n % tiles
        product = lax.dot_general(
            xall[h, :, pl.ds(m * GTILE, GTILE)], gall[...], (((0,), (0,)), ((), ())), preferred_element_type=F32
        )
        rows = pl.ds(n * GTILE, GTILE)
        gwb[rows] = product.astype(BF)

    both = (0, 1)
    pl.semaphore_wait(barrier, len(neighbours))
    for along in (0, 1):
        for h in both:
            for step in (1, -1):
                x_send_own(h, along, step)
    loads["pre"].wait()
    loads["gh"].wait()
    for q in (0, 2, 1, 3):
        g_compute(q)
        g_send(0, q, 1)
        g_send(0, q, -1)
    loads["x0"].wait()
    loads["x1"].wait()
    for h in both:
        x_share(h, 0, 0)
    loads["w"].wait()
    for h in both:
        partial(0, h)
    for o in (3, 1):
        for h in both:
            x_first(h, o)
    for o in (3, 1):
        for h in both:
            x_turn(h, o)
    g_forward(3, 0)
    g_forward(1, 2)
    for h in both:
        x_second(h, 0)
    g_forward(3, 1)
    g_forward(1, 3)
    for h in both:
        x_far(h)
    for h in both:
        x_second(h, 3)
    for q in (2, 3):
        g_arrived(3, q)
    partial(3, 0)
    for h in both:
        x_second(h, 1)
    partial(3, 1)
    for q in (0, 1):
        g_arrived(1, q)
    partial(1, 0)
    for h in both:
        x_last(h, 0)
    partial(1, 1)
    odd = x % 2 == 1
    lead = jnp.logical_and(core == 0, odd)
    lead_own = (x + core) % 2 == 0
    last = jnp.logical_and(core == 1, x % 2 == 0)

    def owned(h, ob):
        return (z + (ob if h == 1 else 2)) % 2 == x // 2

    def first_steps(halves, when):
        for h in halves:
            for ob in (2, 1, 3, 0):
                pl.when(when(h, ob))(functools.partial(first_step, h, ob))

    def first_sends():
        for h in both:
            for ob in (2, 1, 3, 0):
                first_sent(h, ob)

    first_steps(both, lambda h, ob: jnp.logical_and(lead_own, owned(h, ob)))
    pl.when(lead)(lambda: first_steps((0,), lambda h, ob: True))
    for h in both:
        x_second(h, 2)
    for q in range(4):
        g_arrived(2, q)
    partial(2, 0)
    pl.when(lead)(lambda: first_steps((1,), lambda h, ob: True))
    partial(2, 1)
    first_steps(
        both, lambda h, ob: jnp.logical_or(last, jnp.logical_and(lead_own, jnp.logical_not(owned(h, ob))))
    )
    first_sends()
    for ob in (2, 1, 3):
        for h in both:
            second_step(h, ob)
    for o1 in (3, 1, 2):
        for h in both:
            x_last(h, o1)
    for o1 in range(N):
        for o2 in range(N):
            for h in both:
                x_shared(h, o1, o2)
    weight_tile(0)
    weight_tile(1)
    for h in both:
        third_step(h, 2)
        fourth_step(h)
    for h in both:
        second_step(h, 0)
    weight_tile(2)
    weight_tile(3)
    for h in both:
        third_step(h, 1)
        fifth_step_early(h, 0)
    weight_tile(4)
    for h in both:
        third_step(h, 3)
        fifth_step_early(h, 1)
    weight_tile(5)
    for slot in range(PS_SEMS):
        piece = part.at[1, 0, 0, pl.ds(0, CHUNK)]
        pltpu.make_async_remote_copy(
            src_ref=piece, dst_ref=piece, send_sem=ps_s.ref.at[slot], recv_sem=ps_r.ref.at[0],
            device_id=sibling, device_id_type=MESH,
        ).wait_send()
    for h in both:
        for sub in (0, 1):
            fifth_step(h, sub)
    drain(12)
    for h in both:
        third_step(h, 0)
    for h in both:
        sixth_step_early(h)
    for sub in (0, 1):
        for h in both:
            sixth_step(h, sub)
    drain(0)


def write_out(gi, gw, gi_hbm, gw_hbm, sems):
    rows = FEAT // WRITES
    copies = [pltpu.make_async_copy(gi, gi_hbm, sems.at[WRITES])]
    for n in range(WRITES):
        part = pl.ds(n * rows, rows)
        copies.append(pltpu.make_async_copy(gw.at[part], gw_hbm.at[part], sems.at[n]))
    for copy in copies:
        copy.start()
    for copy in copies:
        copy.wait()


def per_device(inputs, weight, pre_act, grad_hidden):
    dma = pltpu.SemaphoreType.DMA
    grads = pl.pallas_call(
        kernel,
        out_shape=(pltpu.VMEM((TOK, FEAT), BF), pltpu.VMEM((FEAT, HID), BF)),
        in_specs=[pl.BlockSpec(memory_space=pl.ANY)] * 4,
        out_specs=(pl.BlockSpec(memory_space=pltpu.VMEM), pl.BlockSpec(memory_space=pltpu.VMEM)),
        scratch_shapes=[
            pltpu.VMEM((2, N * BLOCK, HALF), BF),
            pltpu.VMEM((N * BLOCK, HID), BF),
            pltpu.VMEM((BLOCK, HID), BF),
            pltpu.VMEM((BLOCK, HID), BF),
            pltpu.VMEM((FEAT, HID), BF),
            pltpu.VMEM((2, 2, 2, BLOCK, HALF), BF),
            pltpu.VMEM((2, 2, BLOCK, HALF), BF),
            pltpu.VMEM((2, 2, N, TOK, SUB), BF),
            pltpu.VMEM((2, 2, N, TOK, HALF), BF),
            pltpu.VMEM((2, 2, TOK, SUB), BF),
            pltpu.VMEM((2, 2, TOK, HALF), BF),
            pltpu.VMEM((2, TOK, HALF), F32),
            pltpu.VMEM((2, 2, TOK, SUB), F32),
            dma((64,)), dma((AG_SEMS,)),
            dma((SIB_SEMS,)), dma((SIB_SEMS,)),
            dma((G_SEMS,)), dma((G_SEMS,)),
            dma((PS_SEMS,)), dma((PS_SEMS,)),
            dma((RS_SEMS,)), dma((RS_SEMS,)),
            dma((LOCAL_SEMS,)),
        ],
        compiler_params=pltpu.CompilerParams(
            collective_id=0, has_side_effects=True, vmem_limit_bytes=50 << 20
        ),
        cost_estimate=pl.CostEstimate(flops=14_500_000_000, bytes_accessed=16_000_000, transcendentals=300_000),
        name="gelu_up_backward",
    )(inputs, weight, pre_act, grad_hidden)
    return pl.pallas_call(
        write_out,
        out_shape=tuple(jax.ShapeDtypeStruct(g.shape, g.dtype) for g in grads),
        in_specs=[pl.BlockSpec(memory_space=pltpu.VMEM)] * 2,
        out_specs=[pl.BlockSpec(memory_space=pl.ANY)] * 2,
        scratch_shapes=[dma((1 + WRITES,))],
        compiler_params=pltpu.CompilerParams(vmem_limit_bytes=1 << 20),
        name="write_out",
    )(*(pltpu.with_memory_space_constraint(g, pltpu.VMEM) for g in grads))


def solution(mesh):
    return jax.shard_map(
        per_device,
        mesh=mesh,
        in_specs=(
            P(("depth", "row"), "col"),
            P("col", ("depth", "row")),
            P("col", ("depth", "row")),
            P("col", ("depth", "row")),
        ),
        out_specs=(P(("depth", "row"), "col"), P("col", ("depth", "row"))),
        check_vma=False,
    )
```

```python
import functools
import math

import jax
import jax.numpy as jnp
from jax import lax
from jax.experimental import pallas as pl
from jax.experimental.pallas import tpu as pltpu
from jax.sharding import PartitionSpec as P

MESH = pl.DeviceIdType.MESH
BF, F32 = jnp.bfloat16, jnp.float32

N = 4
TOK = 48
HALF = 1536
SUB = HALF // 2
FEAT = 2 * HALF
HID = 768
BLOCK = 384
CHUNK = 96
GTILE = 512
WRITES = 4


def gelu_slope(pre):
    coeff = math.sqrt(2.0 / math.pi)
    inner = coeff * (pre + 0.044715 * pre * pre * pre)
    tanh_val = jnp.tanh(inner)
    return 0.5 * (1.0 + tanh_val) + 0.5 * pre * (1.0 - tanh_val * tanh_val) * coeff * (
        1.0 + 3.0 * 0.044715 * pre * pre
    )


class Slots:
    def __init__(self, ref, size):
        self.ref, self.size, self.keys = ref, size, {}

    def __getitem__(self, key):
        place = self.keys.setdefault(key, len(self.keys))
        assert place < self.size
        return self.ref.at[place]


AG_SEMS, SIB_SEMS, G_SEMS, PS_SEMS, RS_SEMS, LOCAL_SEMS = 44, 32, 12, 16, 44, 16


def kernel(
    x_hbm, w_hbm, pre_hbm, gh_hbm, gi_ref, gwb,
    xall, gall, pre, gh, w, part, psib, r1, r2, r3, r4, own, onward,
    ag_s, ag_r, sib_s, sib_r, g_s, g_r, ps_s, ps_r, rs_s, rs_r, local,
):
    dep, row, x = lax.axis_index("depth"), lax.axis_index("row"), lax.axis_index("col")
    z_lo, core = dep // 2, dep % 2
    y, z = row // 2, (row % 2) * 2 + z_lo
    place = {"x": x, "y": y, "z": z}

    def device(x, y, z, core):
        return ((z % 2) * 2 + core, y * 2 + z // 2, x)

    def towards(axis, step):
        there = dict(place)
        there[axis] = (place[axis] + step) % N
        return device(there["x"], there["y"], there["z"], core)

    sibling = device(x, y, z, 1 - core)

    ag_s, ag_r = Slots(ag_s, 64), Slots(ag_r, AG_SEMS)
    sib_s, sib_r = Slots(sib_s, SIB_SEMS), Slots(sib_r, SIB_SEMS)
    g_s, g_r = Slots(g_s, G_SEMS), Slots(g_r, G_SEMS)
    ps_s, ps_r = Slots(ps_s, PS_SEMS), Slots(ps_r, PS_SEMS)
    rs_s, rs_r = Slots(rs_s, RS_SEMS), Slots(rs_r, RS_SEMS)
    local = Slots(local, LOCAL_SEMS)

    barrier = pltpu.get_barrier_semaphore()
    neighbours = [sibling] + [towards(axis, step) for axis in "xyz" for step in (1, -1)]
    for there in neighbours:
        pl.semaphore_signal(barrier, inc=1, device_id=there, device_id_type=MESH)

    own_row = pl.multiple_of((dep * 8 + row) * TOK, 16)
    loads = {
        "pre": pltpu.make_async_copy(pre_hbm, pre, local["pre"]),
        "gh": pltpu.make_async_copy(gh_hbm, gh, local["gh"]),
        "x0": pltpu.make_async_copy(x_hbm.at[:, pl.ds(0, HALF)], xall.at[0, pl.ds(own_row, TOK)], local["x0"]),
        "x1": pltpu.make_async_copy(x_hbm.at[:, pl.ds(HALF, HALF)], xall.at[1, pl.ds(own_row, TOK)], local["x1"]),
        "w": pltpu.make_async_copy(w_hbm, w, local["w"]),
    }
    for name in ("x0", "x1", "pre", "gh", "w"):
        loads[name].start()

    pending = []

    def send(src, dst, s, r, there):
        copy = pltpu.make_async_remote_copy(
            src_ref=src, dst_ref=dst, send_sem=s, recv_sem=r, device_id=there, device_id_type=MESH
        )
        copy.start()
        return copy

    def arrived(dst, s, r):
        pltpu.make_async_remote_copy(
            src_ref=dst, dst_ref=dst, send_sem=s, recv_sem=r, device_id=sibling, device_id_type=MESH
        ).wait_recv()

    def drain(left):
        while len(pending) > left:
            pending.pop(0).wait_send()

    axes = (("y", "z"), ("z", "y"))

    def x_rows(h, o1, o2, of_core):
        first, second = (place[axes[h][0]] + o1) % N, (place[axes[h][1]] + o2) % N
        yy, zz = (first, second) if h == 0 else (second, first)
        return pl.multiple_of((((zz % 2) * 2 + of_core) * 8 + yy * 2 + zz // 2) * TOK, 16)

    def x_block(h, o1, o2, sub, of_core):
        rows = pl.ds(x_rows(h, o1, o2, of_core), TOK)
        if sub is None:
            return xall.at[h, rows]
        return xall.at[h, rows, pl.ds(sub * SUB, SUB)]

    def x_send(h, o1, o2, sub, along, step):
        block = x_block(h, o1, o2, sub, core)
        there = ((o1 - step) % N, o2) if along == 0 else (o1, (o2 - step) % N)
        pending.append(
            send(block, block, ag_s[h, o1, o2, sub, along, step], ag_r[(h, *there, sub)], towards(axes[h][along], step))
        )

    def x_send_own(h, along, step):
        there = (-step % N, 0) if along == 0 else (0, -step % N)
        pending.append(send(
            x_hbm.at[:, pl.ds(h * HALF, HALF)], x_block(h, 0, 0, None, core),
            ag_s[h, 0, 0, None, along, step], ag_r[(h, *there, None)], towards(axes[h][along], step),
        ))

    def x_arrived(h, o1, o2, sub):
        arrived(x_block(h, o1, o2, sub, core), ag_s[h, 0, 0, None, 0, 1], ag_r[h, o1, o2, sub])

    def x_share(h, o1, o2):
        block = x_block(h, o1, o2, None, core)
        pending.append(send(block, block, sib_s[h, o1, o2], sib_r[h, o1, o2], sibling))

    def x_shared(h, o1, o2):
        arrived(x_block(h, o1, o2, None, 1 - core), sib_s[h, 0, 0], sib_r[h, o1, o2])

    def x_first(h, o1):
        x_arrived(h, o1, 0, None)
        x_send(h, o1, 0, 0 if o1 == 3 else 1, 0, 1 if o1 == 3 else -1)

    def x_turn(h, o1):
        for step in (1, -1):
            x_send(h, o1, 0, None, 1, step)
        x_share(h, o1, 0)

    def x_far(h):
        for sub in (0, 1):
            x_arrived(h, 2, 0, sub)
            x_send(h, 2, 0, sub, 1, 1)
            x_send(h, 2, 0, sub, 1, -1)
        x_share(h, 2, 0)

    def x_second(h, o1):
        if o1 == 2:
            for o2, sub in ((3, 0), (1, 1)):
                x_arrived(h, 2, o2, sub)
                x_send(h, 2, o2, sub, 1, 1 if o2 == 3 else -1)
            for o2, sub in ((3, 1), (1, 0)):
                x_arrived(h, 2, o2, sub)
                x_share(h, 2, o2)
            return
        for o2 in (3, 1):
            x_arrived(h, o1, o2, None)
            x_send(h, o1, o2, 0 if o2 == 3 else 1, 1, 1 if o2 == 3 else -1)
            x_share(h, o1, o2)

    def x_last(h, o1):
        for sub in (0, 1):
            x_arrived(h, o1, 2, sub)
        x_share(h, o1, 2)

    def g_block(o, q):
        return gall.at[pl.ds(pl.multiple_of(((x + o) % N) * BLOCK + q * CHUNK, 16), CHUNK)]

    def g_send(o, q, step):
        block = g_block(o, q)
        pending.append(send(block, block, g_s[o, q, step], g_r[(o - step) % N, q], towards("x", step)))

    def g_arrived(o, q):
        arrived(g_block(o, q), g_s[0, 0, 1], g_r[o, q])

    def g_forward(o, q):
        g_arrived(o, q)
        g_send(o, q, 1 if o == 3 else -1)

    def g_compute(q):
        @pl.loop(0, CHUNK // 32)
        def _(i):
            rows = pl.ds(pl.multiple_of(q * CHUNK + i * 32, 32), 32)
            slope = gelu_slope(pre[rows].astype(F32))
            value = (gh[rows].astype(F32) * slope).astype(BF)
            gall[pl.ds(pl.multiple_of(x * BLOCK + q * CHUNK + i * 32, 32), 32)] = value

    def partial(o, h):
        block = (x + o) % N
        away, z_of = (block + core) % 2, block // 2
        rows = pl.ds(pl.multiple_of(block * BLOCK, 16), BLOCK)
        @pl.loop(0, 2)
        def _(n):
            product = lax.dot_general(
                gall[rows],
                w[pl.ds(pl.multiple_of(h * HALF + n * SUB, SUB), SUB)],
                (((1,), (1,)), ((), ())),
                preferred_element_type=F32,
            )
            part[away, z_of, h, :, pl.ds(pl.multiple_of(n * SUB, SUB), SUB)] = product.astype(BF)

        @pl.when(away == 1)
        def _():
            for yy in range(N):
                piece = pl.ds(yy * CHUNK, CHUNK)
                slot = (o // 2 * 2 + h) * N + yy
                send(
                    part.at[1, z_of, h, piece], psib.at[z_of, h, piece],
                    ps_s.ref.at[slot], ps_r.ref.at[(z_of * 2 + h) * N + yy], sibling,
                )

    def sib_part(zl, h, yy):
        piece = psib.at[zl, h, pl.ds(pl.multiple_of(yy * CHUNK, 16), CHUNK)]
        arrived(piece, ps_s.ref.at[0], ps_r.ref.at[(zl * 2 + h) * N + yy])

    rs_axes = (("z", "y"), ("y", "z"))

    def target(h, oa, ob):
        a, b = (place[rs_axes[h][0]] + oa) % N, (place[rs_axes[h][1]] + ob) % N
        zz, yy = (a, b) if h == 0 else (b, a)
        return zz % 2, pl.multiple_of(yy * CHUNK + (zz // 2) * TOK, 16), yy

    def rows16(body):
        @pl.loop(0, TOK // 16)
        def _(i):
            body(pl.multiple_of(i * 16, 16))

    def whole(h, zl, row0, i):
        at = pl.ds(pl.multiple_of(row0 + i, 16), 16)
        return part[0, zl, h, at].astype(F32) + psib[zl, h, at].astype(F32)

    def first_step(h, ob):
        zl, row0, yy = target(h, 2, ob)
        if h == 0 or ob in (2, 1):
            sib_part(zl, h, yy)

        def add(i):
            part[0, zl, h, pl.ds(pl.multiple_of(row0 + i, 16), 16)] = whole(h, zl, row0, i).astype(BF)

        rows16(add)
        for sub, step in ((0, 1), (1, -1)):
            send(
                part.at[0, zl, h, pl.ds(row0, TOK), pl.ds(sub * SUB, SUB)], r1.at[h, sub, ob],
                rs_s[1, h, sub, ob], rs_r[1, h, sub, ob], towards(rs_axes[h][0], step),
            )

    def first_sent(h, ob):
        zl, row0, _ = target(h, 2, ob)
        for sub, step in ((0, 1), (1, -1)):
            pending.append(pltpu.make_async_remote_copy(
                src_ref=part.at[0, zl, h, pl.ds(row0, TOK), pl.ds(sub * SUB, SUB)], dst_ref=r1.at[h, sub, ob],
                send_sem=rs_s[1, h, sub, ob], recv_sem=rs_r[1, h, sub, ob],
                device_id=towards(rs_axes[h][0], step), device_id_type=MESH,
            ))

    def second_step(h, ob):
        for sub, oa, step in ((0, 1, 1), (1, 3, -1)):
            zl, row0, yy = target(h, oa, ob)
            if (h == 0 and sub == 0) or (h == 1 and ob in (2, 1)):
                sib_part(zl, h, yy)
            arrived(r1.at[h, sub, ob], rs_s[1, h, sub, ob], rs_r[1, h, sub, ob])
            got, kept = pl.ds(sub * SUB, SUB), pl.ds((1 - sub) * SUB, SUB)

            def add(i):
                at = pl.ds(pl.multiple_of(row0 + i, 16), 16)
                part[0, zl, h, at, got] = (
                    part[0, zl, h, at, got].astype(F32) + psib[zl, h, at, got].astype(F32)
                    + r1[h, sub, ob, pl.ds(i, 16)].astype(F32)
                ).astype(BF)
                part[0, zl, h, at, kept] = (
                    part[0, zl, h, at, kept].astype(F32) + psib[zl, h, at, kept].astype(F32)
                ).astype(BF)

            rows16(add)
            pending.append(send(
                part.at[0, zl, h, pl.ds(row0, TOK)], r2.at[h, sub, ob],
                rs_s[2, h, sub, ob], rs_r[2, h, sub, ob], towards(rs_axes[h][0], step),
            ))

    def third_step(h, ob):
        zl, row0, yy = target(h, 0, ob)
        if h == 1 and ob in (2, 1):
            sib_part(zl, h, yy)
        for sub in (0, 1):
            arrived(r2.at[h, sub, ob], rs_s[2, h, sub, ob], rs_r[2, h, sub, ob])

        def add(i):
            at, here = pl.ds(i, 16), pl.ds(pl.multiple_of(row0 + i, 16), 16)
            total = whole(h, zl, row0, i) + r2[h, 0, ob, at].astype(F32) + r2[h, 1, ob, at].astype(F32)
            if ob == 0:
                own[h, at] = total
            elif ob == 2:
                part[0, zl, h, here] = total.astype(BF)
            else:
                sub = 0 if ob == 1 else 1
                onward[h, sub, at] = total[:, sub * SUB:(sub + 1) * SUB]
                part[0, zl, h, here, pl.ds((1 - sub) * SUB, SUB)] = (
                    total[:, (1 - sub) * SUB:(2 - sub) * SUB].astype(BF)
                )

        rows16(add)

    def fourth_step(h):
        zl, row0, _ = target(h, 0, 2)
        for sub, step in ((0, 1), (1, -1)):
            pending.append(send(
                part.at[0, zl, h, pl.ds(row0, TOK), pl.ds(sub * SUB, SUB)], r3.at[h, sub],
                rs_s[3, h, sub], rs_r[3, h, sub], towards(rs_axes[h][1], step),
            ))

    def fifth_step_early(h, sub):
        ob, step = ((1, 1), (3, -1))[sub]
        zl, row0, _ = target(h, 0, ob)
        kept = pl.ds((1 - sub) * SUB, SUB)
        pending.append(send(
            part.at[0, zl, h, pl.ds(row0, TOK), kept], r4.at[h, sub, :, kept],
            rs_s[4, h, sub, 1], rs_r[4, h, sub, 1], towards(rs_axes[h][1], step),
        ))

    def fifth_step(h, sub):
        ob, step = ((1, 1), (3, -1))[sub]
        zl, row0, _ = target(h, 0, ob)
        got = pl.ds(sub * SUB, SUB)
        arrived(r3.at[h, sub], rs_s[3, h, sub], rs_r[3, h, sub])

        def add(i):
            at = pl.ds(i, 16)
            part[0, zl, h, pl.ds(pl.multiple_of(row0 + i, 16), 16), got] = (
                onward[h, sub, at] + r3[h, sub, at].astype(F32)
            ).astype(BF)

        rows16(add)
        pending.append(send(
            part.at[0, zl, h, pl.ds(row0, TOK), got], r4.at[h, sub, :, got],
            rs_s[4, h, sub, 0], rs_r[4, h, sub, 0], towards(rs_axes[h][1], step),
        ))

    def sixth_step_early(h):
        for sub in (0, 1):
            kept = pl.ds((1 - sub) * SUB, SUB)
            arrived(r4.at[h, sub, :, kept], rs_s[4, h, sub, 1], rs_r[4, h, sub, 1])

            def add(i):
                at = pl.ds(i, 16)
                own[h, at, kept] = own[h, at, kept] + r4[h, sub, at, kept].astype(F32)

            rows16(add)

    def sixth_step(h, sub):
        got = pl.ds(sub * SUB, SUB)
        arrived(r4.at[h, sub, :, got], rs_s[4, h, sub, 0], rs_r[4, h, sub, 0])

        def add(i):
            at = pl.ds(i, 16)
            gi_ref[at, pl.ds(h * HALF + sub * SUB, SUB)] = (
                own[h, at, got] + r4[h, sub, at, got].astype(F32)
            ).astype(BF)

        rows16(add)

    tiles = HALF // GTILE

    def weight_tile(n):
        h, m = n // tiles, n % tiles
        product = lax.dot_general(
            xall[h, :, pl.ds(m * GTILE, GTILE)], gall[...], (((0,), (0,)), ((), ())), preferred_element_type=F32
        )
        rows = pl.ds(n * GTILE, GTILE)
        gwb[rows] = product.astype(BF)

    both = (0, 1)
    pl.semaphore_wait(barrier, len(neighbours))
    for along in (0, 1):
        for h in both:
            for step in (1, -1):
                x_send_own(h, along, step)
    loads["pre"].wait()
    loads["gh"].wait()
    for q in (0, 2, 1, 3):
        g_compute(q)
        g_send(0, q, 1)
        g_send(0, q, -1)
    loads["x0"].wait()
    loads["x1"].wait()
    for h in both:
        x_share(h, 0, 0)
    loads["w"].wait()
    for h in both:
        partial(0, h)
    for o in (3, 1):
        for h in both:
            x_first(h, o)
    for o in (3, 1):
        for h in both:
            x_turn(h, o)
    g_forward(3, 0)
    g_forward(1, 2)
    for h in both:
        x_second(h, 0)
    g_forward(3, 1)
    g_forward(1, 3)
    for h in both:
        x_far(h)
    for h in both:
        x_second(h, 3)
    for q in (2, 3):
        g_arrived(3, q)
    partial(3, 0)
    for h in both:
        x_second(h, 1)
    partial(3, 1)
    for q in (0, 1):
        g_arrived(1, q)
    partial(1, 0)
    for h in both:
        x_last(h, 0)
    partial(1, 1)
    odd = x % 2 == 1
    lead = jnp.logical_and(core == 0, odd)
    lead_own = (x + core) % 2 == 0
    last = jnp.logical_and(core == 1, x % 2 == 0)

    def owned(h, ob):
        return (z + (ob if h == 1 else 2)) % 2 == x // 2

    def first_steps(halves, when):
        for h in halves:
            for ob in (2, 1, 3, 0):
                pl.when(when(h, ob))(functools.partial(first_step, h, ob))

    def first_sends():
        for h in both:
            for ob in (2, 1, 3, 0):
                first_sent(h, ob)

    for h in both:
        x_second(h, 2)
    first_steps(both, lambda h, ob: jnp.logical_and(lead_own, owned(h, ob)))
    pl.when(jnp.logical_not(lead_own))(lambda: first_steps((0,), lambda h, ob: True))
    for q in range(4):
        g_arrived(2, q)
    partial(2, 0)
    pl.when(lead)(lambda: first_steps((1,), lambda h, ob: True))
    partial(2, 1)
    pl.when(last)(lambda: first_steps((1,), lambda h, ob: True))
    first_steps(both, lambda h, ob: jnp.logical_and(lead_own, jnp.logical_not(owned(h, ob))))
    first_sends()
    for ob in (2, 1, 3):
        for h in both:
            second_step(h, ob)
    for o1 in (3, 1, 2):
        for h in both:
            x_last(h, o1)
    for o1 in range(N):
        for o2 in range(N):
            for h in both:
                x_shared(h, o1, o2)
    weight_tile(0)
    weight_tile(1)
    for h in both:
        third_step(h, 2)
        fourth_step(h)
    for h in both:
        second_step(h, 0)
    weight_tile(2)
    weight_tile(3)
    for h in both:
        third_step(h, 1)
        fifth_step_early(h, 0)
    weight_tile(4)
    for h in both:
        third_step(h, 3)
        fifth_step_early(h, 1)
    weight_tile(5)
    for slot in range(PS_SEMS):
        piece = part.at[1, 0, 0, pl.ds(0, CHUNK)]
        pltpu.make_async_remote_copy(
            src_ref=piece, dst_ref=piece, send_sem=ps_s.ref.at[slot], recv_sem=ps_r.ref.at[0],
            device_id=sibling, device_id_type=MESH,
        ).wait_send()
    for h in both:
        for sub in (0, 1):
            fifth_step(h, sub)
    drain(12)
    for h in both:
        third_step(h, 0)
    for h in both:
        sixth_step_early(h)
    for sub in (0, 1):
        for h in both:
            sixth_step(h, sub)
    drain(0)


def write_out(gi, gw, gi_hbm, gw_hbm, sems):
    rows = FEAT // WRITES
    copies = [pltpu.make_async_copy(gi, gi_hbm, sems.at[WRITES])]
    for n in range(WRITES):
        part = pl.ds(n * rows, rows)
        copies.append(pltpu.make_async_copy(gw.at[part], gw_hbm.at[part], sems.at[n]))
    for copy in copies:
        copy.start()
    for copy in copies:
        copy.wait()


def per_device(inputs, weight, pre_act, grad_hidden):
    dma = pltpu.SemaphoreType.DMA
    grads = pl.pallas_call(
        kernel,
        out_shape=(pltpu.VMEM((TOK, FEAT), BF), pltpu.VMEM((FEAT, HID), BF)),
        in_specs=[pl.BlockSpec(memory_space=pl.ANY)] * 4,
        out_specs=(pl.BlockSpec(memory_space=pltpu.VMEM), pl.BlockSpec(memory_space=pltpu.VMEM)),
        scratch_shapes=[
            pltpu.VMEM((2, N * BLOCK, HALF), BF),
            pltpu.VMEM((N * BLOCK, HID), BF),
            pltpu.VMEM((BLOCK, HID), BF),
            pltpu.VMEM((BLOCK, HID), BF),
            pltpu.VMEM((FEAT, HID), BF),
            pltpu.VMEM((2, 2, 2, BLOCK, HALF), BF),
            pltpu.VMEM((2, 2, BLOCK, HALF), BF),
            pltpu.VMEM((2, 2, N, TOK, SUB), BF),
            pltpu.VMEM((2, 2, N, TOK, HALF), BF),
            pltpu.VMEM((2, 2, TOK, SUB), BF),
            pltpu.VMEM((2, 2, TOK, HALF), BF),
            pltpu.VMEM((2, TOK, HALF), F32),
            pltpu.VMEM((2, 2, TOK, SUB), F32),
            dma((64,)), dma((AG_SEMS,)),
            dma((SIB_SEMS,)), dma((SIB_SEMS,)),
            dma((G_SEMS,)), dma((G_SEMS,)),
            dma((PS_SEMS,)), dma((PS_SEMS,)),
            dma((RS_SEMS,)), dma((RS_SEMS,)),
            dma((LOCAL_SEMS,)),
        ],
        compiler_params=pltpu.CompilerParams(
            collective_id=0, has_side_effects=True, vmem_limit_bytes=50 << 20
        ),
        cost_estimate=pl.CostEstimate(flops=14_500_000_000, bytes_accessed=16_000_000, transcendentals=300_000),
        name="gelu_up_backward",
    )(inputs, weight, pre_act, grad_hidden)
    return pl.pallas_call(
        write_out,
        out_shape=tuple(jax.ShapeDtypeStruct(g.shape, g.dtype) for g in grads),
        in_specs=[pl.BlockSpec(memory_space=pltpu.VMEM)] * 2,
        out_specs=[pl.BlockSpec(memory_space=pl.ANY)] * 2,
        scratch_shapes=[dma((1 + WRITES,))],
        compiler_params=pltpu.CompilerParams(vmem_limit_bytes=1 << 20),
        name="write_out",
    )(*(pltpu.with_memory_space_constraint(g, pltpu.VMEM) for g in grads))


def solution(mesh):
    return jax.shard_map(
        per_device,
        mesh=mesh,
        in_specs=(
            P(("depth", "row"), "col"),
            P("col", ("depth", "row")),
            P("col", ("depth", "row")),
            P("col", ("depth", "row")),
        ),
        out_specs=(P(("depth", "row"), "col"), P("col", ("depth", "row"))),
        check_vma=False,
    )
```

```python
import functools
import math

import jax
import jax.numpy as jnp
from jax import lax
from jax.experimental import pallas as pl
from jax.experimental.pallas import tpu as pltpu
from jax.sharding import PartitionSpec as P

MESH = pl.DeviceIdType.MESH
BF, F32 = jnp.bfloat16, jnp.float32

N = 4
TOK = 48
HALF = 1536
SUB = HALF // 2
FEAT = 2 * HALF
HID = 768
BLOCK = 384
CHUNK = 96
GTILE = 512
WRITES = 4


def gelu_slope(pre):
    coeff = math.sqrt(2.0 / math.pi)
    inner = coeff * (pre + 0.044715 * pre * pre * pre)
    tanh_val = jnp.tanh(inner)
    return 0.5 * (1.0 + tanh_val) + 0.5 * pre * (1.0 - tanh_val * tanh_val) * coeff * (
        1.0 + 3.0 * 0.044715 * pre * pre
    )


class Slots:
    def __init__(self, ref, size):
        self.ref, self.size, self.keys = ref, size, {}

    def __getitem__(self, key):
        place = self.keys.setdefault(key, len(self.keys))
        assert place < self.size
        return self.ref.at[place]


AG_SEMS, SIB_SEMS, G_SEMS, PS_SEMS, RS_SEMS, LOCAL_SEMS = 44, 32, 12, 16, 44, 16


def kernel(
    x_hbm, w_hbm, pre_hbm, gh_hbm, gi_ref, gwb,
    xall, gall, pre, gh, w, part, psib, r1, r2, r3, r4, own, onward,
    ag_s, ag_r, sib_s, sib_r, g_s, g_r, ps_s, ps_r, rs_s, rs_r, local,
):
    dep, row, x = lax.axis_index("depth"), lax.axis_index("row"), lax.axis_index("col")
    z_lo, core = dep // 2, dep % 2
    y, z = row // 2, (row % 2) * 2 + z_lo
    place = {"x": x, "y": y, "z": z}

    def device(x, y, z, core):
        return ((z % 2) * 2 + core, y * 2 + z // 2, x)

    def towards(axis, step):
        there = dict(place)
        there[axis] = (place[axis] + step) % N
        return device(there["x"], there["y"], there["z"], core)

    sibling = device(x, y, z, 1 - core)

    ag_s, ag_r = Slots(ag_s, 64), Slots(ag_r, AG_SEMS)
    sib_s, sib_r = Slots(sib_s, SIB_SEMS), Slots(sib_r, SIB_SEMS)
    g_s, g_r = Slots(g_s, G_SEMS), Slots(g_r, G_SEMS)
    ps_s, ps_r = Slots(ps_s, PS_SEMS), Slots(ps_r, PS_SEMS)
    rs_s, rs_r = Slots(rs_s, RS_SEMS), Slots(rs_r, RS_SEMS)
    local = Slots(local, LOCAL_SEMS)

    barrier = pltpu.get_barrier_semaphore()
    neighbours = [sibling] + [towards(axis, step) for axis in "xyz" for step in (1, -1)]
    for there in neighbours:
        pl.semaphore_signal(barrier, inc=1, device_id=there, device_id_type=MESH)

    own_row = pl.multiple_of((dep * 8 + row) * TOK, 16)
    loads = {
        "pre": pltpu.make_async_copy(pre_hbm, pre, local["pre"]),
        "gh": pltpu.make_async_copy(gh_hbm, gh, local["gh"]),
        "x0": pltpu.make_async_copy(x_hbm.at[:, pl.ds(0, HALF)], xall.at[0, pl.ds(own_row, TOK)], local["x0"]),
        "x1": pltpu.make_async_copy(x_hbm.at[:, pl.ds(HALF, HALF)], xall.at[1, pl.ds(own_row, TOK)], local["x1"]),
        "w": pltpu.make_async_copy(w_hbm, w, local["w"]),
    }
    for name in ("x0", "x1", "pre", "gh", "w"):
        loads[name].start()

    pending = []

    def send(src, dst, s, r, there):
        copy = pltpu.make_async_remote_copy(
            src_ref=src, dst_ref=dst, send_sem=s, recv_sem=r, device_id=there, device_id_type=MESH
        )
        copy.start()
        return copy

    def arrived(dst, s, r):
        pltpu.make_async_remote_copy(
            src_ref=dst, dst_ref=dst, send_sem=s, recv_sem=r, device_id=sibling, device_id_type=MESH
        ).wait_recv()

    def drain(left):
        while len(pending) > left:
            pending.pop(0).wait_send()

    axes = (("y", "z"), ("z", "y"))

    def x_rows(h, o1, o2, of_core):
        first, second = (place[axes[h][0]] + o1) % N, (place[axes[h][1]] + o2) % N
        yy, zz = (first, second) if h == 0 else (second, first)
        return pl.multiple_of((((zz % 2) * 2 + of_core) * 8 + yy * 2 + zz // 2) * TOK, 16)

    def x_block(h, o1, o2, sub, of_core):
        rows = pl.ds(x_rows(h, o1, o2, of_core), TOK)
        if sub is None:
            return xall.at[h, rows]
        return xall.at[h, rows, pl.ds(sub * SUB, SUB)]

    def x_send(h, o1, o2, sub, along, step):
        block = x_block(h, o1, o2, sub, core)
        there = ((o1 - step) % N, o2) if along == 0 else (o1, (o2 - step) % N)
        pending.append(
            send(block, block, ag_s[h, o1, o2, sub, along, step], ag_r[(h, *there, sub)], towards(axes[h][along], step))
        )

    def x_send_own(h, along, step):
        there = (-step % N, 0) if along == 0 else (0, -step % N)
        pending.append(send(
            x_hbm.at[:, pl.ds(h * HALF, HALF)], x_block(h, 0, 0, None, core),
            ag_s[h, 0, 0, None, along, step], ag_r[(h, *there, None)], towards(axes[h][along], step),
        ))

    def x_arrived(h, o1, o2, sub):
        arrived(x_block(h, o1, o2, sub, core), ag_s[h, 0, 0, None, 0, 1], ag_r[h, o1, o2, sub])

    def x_share(h, o1, o2):
        block = x_block(h, o1, o2, None, core)
        pending.append(send(block, block, sib_s[h, o1, o2], sib_r[h, o1, o2], sibling))

    def x_shared(h, o1, o2):
        arrived(x_block(h, o1, o2, None, 1 - core), sib_s[h, 0, 0], sib_r[h, o1, o2])

    def x_first(h, o1):
        x_arrived(h, o1, 0, None)
        x_send(h, o1, 0, 0 if o1 == 3 else 1, 0, 1 if o1 == 3 else -1)

    def x_turn(h, o1):
        for step in (1, -1):
            x_send(h, o1, 0, None, 1, step)
        x_share(h, o1, 0)

    def x_far(h):
        for sub in (0, 1):
            x_arrived(h, 2, 0, sub)
            x_send(h, 2, 0, sub, 1, 1)
            x_send(h, 2, 0, sub, 1, -1)
        x_share(h, 2, 0)

    def x_second(h, o1):
        if o1 == 2:
            for o2, sub in ((3, 0), (1, 1)):
                x_arrived(h, 2, o2, sub)
                x_send(h, 2, o2, sub, 1, 1 if o2 == 3 else -1)
            for o2, sub in ((3, 1), (1, 0)):
                x_arrived(h, 2, o2, sub)
                x_share(h, 2, o2)
            return
        for o2 in (3, 1):
            x_arrived(h, o1, o2, None)
            x_send(h, o1, o2, 0 if o2 == 3 else 1, 1, 1 if o2 == 3 else -1)
            x_share(h, o1, o2)

    def x_last(h, o1):
        for sub in (0, 1):
            x_arrived(h, o1, 2, sub)
        x_share(h, o1, 2)

    def g_block(o, q):
        return gall.at[pl.ds(pl.multiple_of(((x + o) % N) * BLOCK + q * CHUNK, 16), CHUNK)]

    def g_send(o, q, step):
        block = g_block(o, q)
        pending.append(send(block, block, g_s[o, q, step], g_r[(o - step) % N, q], towards("x", step)))

    def g_arrived(o, q):
        arrived(g_block(o, q), g_s[0, 0, 1], g_r[o, q])

    def g_forward(o, q):
        g_arrived(o, q)
        g_send(o, q, 1 if o == 3 else -1)

    def g_compute(q):
        @pl.loop(0, CHUNK // 32)
        def _(i):
            rows = pl.ds(pl.multiple_of(q * CHUNK + i * 32, 32), 32)
            slope = gelu_slope(pre[rows].astype(F32))
            value = (gh[rows].astype(F32) * slope).astype(BF)
            gall[pl.ds(pl.multiple_of(x * BLOCK + q * CHUNK + i * 32, 32), 32)] = value

    def partial(o, h):
        block = (x + o) % N
        away, z_of = (block + core) % 2, block // 2
        rows = pl.ds(pl.multiple_of(block * BLOCK, 16), BLOCK)
        @pl.loop(0, 2)
        def _(n):
            product = lax.dot_general(
                gall[rows],
                w[pl.ds(pl.multiple_of(h * HALF + n * SUB, SUB), SUB)],
                (((1,), (1,)), ((), ())),
                preferred_element_type=F32,
            )
            part[away, z_of, h, :, pl.ds(pl.multiple_of(n * SUB, SUB), SUB)] = product.astype(BF)

        @pl.when(away == 1)
        def _():
            for yy in range(N):
                piece = pl.ds(yy * CHUNK, CHUNK)
                slot = (o // 2 * 2 + h) * N + yy
                send(
                    part.at[1, z_of, h, piece], psib.at[z_of, h, piece],
                    ps_s.ref.at[slot], ps_r.ref.at[(z_of * 2 + h) * N + yy], sibling,
                )

    def sib_part(zl, h, yy):
        piece = psib.at[zl, h, pl.ds(pl.multiple_of(yy * CHUNK, 16), CHUNK)]
        arrived(piece, ps_s.ref.at[0], ps_r.ref.at[(zl * 2 + h) * N + yy])

    rs_axes = (("z", "y"), ("y", "z"))

    def target(h, oa, ob):
        a, b = (place[rs_axes[h][0]] + oa) % N, (place[rs_axes[h][1]] + ob) % N
        zz, yy = (a, b) if h == 0 else (b, a)
        return zz % 2, pl.multiple_of(yy * CHUNK + (zz // 2) * TOK, 16), yy

    def rows16(body):
        @pl.loop(0, TOK // 16)
        def _(i):
            body(pl.multiple_of(i * 16, 16))

    def whole(h, zl, row0, i):
        at = pl.ds(pl.multiple_of(row0 + i, 16), 16)
        return part[0, zl, h, at].astype(F32) + psib[zl, h, at].astype(F32)

    def first_step(h, ob):
        zl, row0, yy = target(h, 2, ob)
        if h == 0 or ob in (2, 1):
            sib_part(zl, h, yy)

        def add(i):
            part[0, zl, h, pl.ds(pl.multiple_of(row0 + i, 16), 16)] = whole(h, zl, row0, i).astype(BF)

        rows16(add)
        for sub, step in ((0, 1), (1, -1)):
            send(
                part.at[0, zl, h, pl.ds(row0, TOK), pl.ds(sub * SUB, SUB)], r1.at[h, sub, ob],
                rs_s[1, h, sub, ob], rs_r[1, h, sub, ob], towards(rs_axes[h][0], step),
            )

    def first_sent(h, ob):
        zl, row0, _ = target(h, 2, ob)
        for sub, step in ((0, 1), (1, -1)):
            pending.append(pltpu.make_async_remote_copy(
                src_ref=part.at[0, zl, h, pl.ds(row0, TOK), pl.ds(sub * SUB, SUB)], dst_ref=r1.at[h, sub, ob],
                send_sem=rs_s[1, h, sub, ob], recv_sem=rs_r[1, h, sub, ob],
                device_id=towards(rs_axes[h][0], step), device_id_type=MESH,
            ))

    def second_step(h, ob):
        for sub, oa, step in ((0, 1, 1), (1, 3, -1)):
            zl, row0, yy = target(h, oa, ob)
            if (h == 0 and sub == 0) or (h == 1 and ob in (2, 1)):
                sib_part(zl, h, yy)
            arrived(r1.at[h, sub, ob], rs_s[1, h, sub, ob], rs_r[1, h, sub, ob])
            got, kept = pl.ds(sub * SUB, SUB), pl.ds((1 - sub) * SUB, SUB)

            def add(i):
                at = pl.ds(pl.multiple_of(row0 + i, 16), 16)
                part[0, zl, h, at, got] = (
                    part[0, zl, h, at, got].astype(F32) + psib[zl, h, at, got].astype(F32)
                    + r1[h, sub, ob, pl.ds(i, 16)].astype(F32)
                ).astype(BF)
                part[0, zl, h, at, kept] = (
                    part[0, zl, h, at, kept].astype(F32) + psib[zl, h, at, kept].astype(F32)
                ).astype(BF)

            rows16(add)
            pending.append(send(
                part.at[0, zl, h, pl.ds(row0, TOK)], r2.at[h, sub, ob],
                rs_s[2, h, sub, ob], rs_r[2, h, sub, ob], towards(rs_axes[h][0], step),
            ))

    def third_step(h, ob):
        zl, row0, yy = target(h, 0, ob)
        if h == 1 and ob in (2, 1):
            sib_part(zl, h, yy)
        for sub in (0, 1):
            arrived(r2.at[h, sub, ob], rs_s[2, h, sub, ob], rs_r[2, h, sub, ob])

        def add(i):
            at, here = pl.ds(i, 16), pl.ds(pl.multiple_of(row0 + i, 16), 16)
            total = whole(h, zl, row0, i) + r2[h, 0, ob, at].astype(F32) + r2[h, 1, ob, at].astype(F32)
            if ob == 0:
                own[h, at] = total
            elif ob == 2:
                part[0, zl, h, here] = total.astype(BF)
            else:
                sub = 0 if ob == 1 else 1
                onward[h, sub, at] = total[:, sub * SUB:(sub + 1) * SUB]
                part[0, zl, h, here, pl.ds((1 - sub) * SUB, SUB)] = (
                    total[:, (1 - sub) * SUB:(2 - sub) * SUB].astype(BF)
                )

        rows16(add)

    def fourth_step(h):
        zl, row0, _ = target(h, 0, 2)
        for sub, step in ((0, 1), (1, -1)):
            pending.append(send(
                part.at[0, zl, h, pl.ds(row0, TOK), pl.ds(sub * SUB, SUB)], r3.at[h, sub],
                rs_s[3, h, sub], rs_r[3, h, sub], towards(rs_axes[h][1], step),
            ))

    def fifth_step_early(h, sub):
        ob, step = ((1, 1), (3, -1))[sub]
        zl, row0, _ = target(h, 0, ob)
        kept = pl.ds((1 - sub) * SUB, SUB)
        pending.append(send(
            part.at[0, zl, h, pl.ds(row0, TOK), kept], r4.at[h, sub, :, kept],
            rs_s[4, h, sub, 1], rs_r[4, h, sub, 1], towards(rs_axes[h][1], step),
        ))

    def fifth_step(h, sub):
        ob, step = ((1, 1), (3, -1))[sub]
        zl, row0, _ = target(h, 0, ob)
        got = pl.ds(sub * SUB, SUB)
        arrived(r3.at[h, sub], rs_s[3, h, sub], rs_r[3, h, sub])

        def add(i):
            at = pl.ds(i, 16)
            part[0, zl, h, pl.ds(pl.multiple_of(row0 + i, 16), 16), got] = (
                onward[h, sub, at] + r3[h, sub, at].astype(F32)
            ).astype(BF)

        rows16(add)
        pending.append(send(
            part.at[0, zl, h, pl.ds(row0, TOK), got], r4.at[h, sub, :, got],
            rs_s[4, h, sub, 0], rs_r[4, h, sub, 0], towards(rs_axes[h][1], step),
        ))

    def sixth_step_early(h):
        for sub in (0, 1):
            kept = pl.ds((1 - sub) * SUB, SUB)
            arrived(r4.at[h, sub, :, kept], rs_s[4, h, sub, 1], rs_r[4, h, sub, 1])

            def add(i):
                at = pl.ds(i, 16)
                own[h, at, kept] = own[h, at, kept] + r4[h, sub, at, kept].astype(F32)

            rows16(add)

    def sixth_step(h, sub):
        got = pl.ds(sub * SUB, SUB)
        arrived(r4.at[h, sub, :, got], rs_s[4, h, sub, 0], rs_r[4, h, sub, 0])

        def add(i):
            at = pl.ds(i, 16)
            gi_ref[at, pl.ds(h * HALF + sub * SUB, SUB)] = (
                own[h, at, got] + r4[h, sub, at, got].astype(F32)
            ).astype(BF)

        rows16(add)

    tiles = HALF // GTILE

    def weight_tile(n):
        h, m = n // tiles, n % tiles
        product = lax.dot_general(
            xall[h, :, pl.ds(m * GTILE, GTILE)], gall[...], (((0,), (0,)), ((), ())), preferred_element_type=F32
        )
        rows = pl.ds(n * GTILE, GTILE)
        gwb[rows] = product.astype(BF)

    both = (0, 1)
    pl.semaphore_wait(barrier, len(neighbours))
    for along in (0, 1):
        for h in both:
            for step in (1, -1):
                x_send_own(h, along, step)
    loads["pre"].wait()
    loads["gh"].wait()
    for q in (0, 2, 1, 3):
        g_compute(q)
        g_send(0, q, 1)
        g_send(0, q, -1)
    loads["x0"].wait()
    loads["x1"].wait()
    for h in both:
        x_share(h, 0, 0)
    loads["w"].wait()
    for h in both:
        partial(0, h)
    for o in (3, 1):
        for h in both:
            x_first(h, o)
    for o in (3, 1):
        for h in both:
            x_turn(h, o)
    g_forward(3, 0)
    g_forward(1, 2)
    for h in both:
        x_second(h, 0)
    g_forward(3, 1)
    g_forward(1, 3)
    for h in both:
        x_far(h)
    for h in both:
        x_second(h, 3)
    for q in (2, 3):
        g_arrived(3, q)
    partial(3, 0)
    for h in both:
        x_second(h, 1)
    partial(3, 1)
    for q in (0, 1):
        g_arrived(1, q)
    partial(1, 0)
    for h in both:
        x_last(h, 0)
    partial(1, 1)
    odd = x % 2 == 1
    lead = jnp.logical_and(core == 0, odd)
    lead_own = (x + core) % 2 == 0
    last = jnp.logical_and(core == 1, x % 2 == 0)

    def owned(h, ob):
        return (z + (ob if h == 1 else 2)) % 2 == x // 2

    def first_steps(halves, when):
        for h in halves:
            for ob in (2, 1, 3, 0):
                pl.when(when(h, ob))(functools.partial(first_step, h, ob))

    def first_sends():
        for h in both:
            for ob in (2, 1, 3, 0):
                first_sent(h, ob)

    first_steps(both, lambda h, ob: jnp.logical_and(lead_own, owned(h, ob)))
    pl.when(lead)(lambda: first_steps((0,), lambda h, ob: True))
    for q in range(4):
        g_arrived(2, q)
    partial(2, 0)
    for h in both:
        x_second(h, 2)
    pl.when(lead)(lambda: first_steps((1,), lambda h, ob: True))
    partial(2, 1)
    first_steps(
        both, lambda h, ob: jnp.logical_or(last, jnp.logical_and(lead_own, jnp.logical_not(owned(h, ob))))
    )
    first_sends()
    for ob in (2, 1, 3):
        for h in both:
            second_step(h, ob)
    for o1 in (3, 1, 2):
        for h in both:
            x_last(h, o1)
    for o1 in range(N):
        for o2 in range(N):
            for h in both:
                x_shared(h, o1, o2)
    weight_tile(0)
    weight_tile(1)
    for h in both:
        third_step(h, 2)
        fourth_step(h)
    for h in both:
        second_step(h, 0)
    weight_tile(2)
    weight_tile(3)
    for h in both:
        third_step(h, 1)
        fifth_step_early(h, 0)
    weight_tile(4)
    for h in both:
        third_step(h, 3)
        fifth_step_early(h, 1)
    weight_tile(5)
    for slot in range(PS_SEMS):
        piece = part.at[1, 0, 0, pl.ds(0, CHUNK)]
        pltpu.make_async_remote_copy(
            src_ref=piece, dst_ref=piece, send_sem=ps_s.ref.at[slot], recv_sem=ps_r.ref.at[0],
            device_id=sibling, device_id_type=MESH,
        ).wait_send()
    for h in both:
        for sub in (0, 1):
            fifth_step(h, sub)
    drain(12)
    for h in both:
        third_step(h, 0)
    for h in both:
        sixth_step_early(h)
    for sub in (0, 1):
        for h in both:
            sixth_step(h, sub)
    drain(0)


def write_out(gi, gw, gi_hbm, gw_hbm, sems):
    rows = FEAT // WRITES
    copies = [pltpu.make_async_copy(gi, gi_hbm, sems.at[WRITES])]
    for n in range(WRITES):
        part = pl.ds(n * rows, rows)
        copies.append(pltpu.make_async_copy(gw.at[part], gw_hbm.at[part], sems.at[n]))
    for copy in copies:
        copy.start()
    for copy in copies:
        copy.wait()


def per_device(inputs, weight, pre_act, grad_hidden):
    dma = pltpu.SemaphoreType.DMA
    grads = pl.pallas_call(
        kernel,
        out_shape=(pltpu.VMEM((TOK, FEAT), BF), pltpu.VMEM((FEAT, HID), BF)),
        in_specs=[pl.BlockSpec(memory_space=pl.ANY)] * 4,
        out_specs=(pl.BlockSpec(memory_space=pltpu.VMEM), pl.BlockSpec(memory_space=pltpu.VMEM)),
        scratch_shapes=[
            pltpu.VMEM((2, N * BLOCK, HALF), BF),
            pltpu.VMEM((N * BLOCK, HID), BF),
            pltpu.VMEM((BLOCK, HID), BF),
            pltpu.VMEM((BLOCK, HID), BF),
            pltpu.VMEM((FEAT, HID), BF),
            pltpu.VMEM((2, 2, 2, BLOCK, HALF), BF),
            pltpu.VMEM((2, 2, BLOCK, HALF), BF),
            pltpu.VMEM((2, 2, N, TOK, SUB), BF),
            pltpu.VMEM((2, 2, N, TOK, HALF), BF),
            pltpu.VMEM((2, 2, TOK, SUB), BF),
            pltpu.VMEM((2, 2, TOK, HALF), BF),
            pltpu.VMEM((2, TOK, HALF), F32),
            pltpu.VMEM((2, 2, TOK, SUB), F32),
            dma((64,)), dma((AG_SEMS,)),
            dma((SIB_SEMS,)), dma((SIB_SEMS,)),
            dma((G_SEMS,)), dma((G_SEMS,)),
            dma((PS_SEMS,)), dma((PS_SEMS,)),
            dma((RS_SEMS,)), dma((RS_SEMS,)),
            dma((LOCAL_SEMS,)),
        ],
        compiler_params=pltpu.CompilerParams(
            collective_id=0, has_side_effects=True, vmem_limit_bytes=50 << 20
        ),
        cost_estimate=pl.CostEstimate(flops=14_500_000_000, bytes_accessed=16_000_000, transcendentals=300_000),
        name="gelu_up_backward",
    )(inputs, weight, pre_act, grad_hidden)
    return pl.pallas_call(
        write_out,
        out_shape=tuple(jax.ShapeDtypeStruct(g.shape, g.dtype) for g in grads),
        in_specs=[pl.BlockSpec(memory_space=pltpu.VMEM)] * 2,
        out_specs=[pl.BlockSpec(memory_space=pl.ANY)] * 2,
        scratch_shapes=[dma((1 + WRITES,))],
        compiler_params=pltpu.CompilerParams(vmem_limit_bytes=1 << 20),
        name="write_out",
    )(*(pltpu.with_memory_space_constraint(g, pltpu.VMEM) for g in grads))


def solution(mesh):
    return jax.shard_map(
        per_device,
        mesh=mesh,
        in_specs=(
            P(("depth", "row"), "col"),
            P("col", ("depth", "row")),
            P("col", ("depth", "row")),
            P("col", ("depth", "row")),
        ),
        out_specs=(P(("depth", "row"), "col"), P("col", ("depth", "row"))),
        check_vma=False,
    )
```
